32 devices in a mesh: batch: 4 (over y, x), slab: 8 (over z, core).
Axes of the slice: x: 2, y: 2, z: 4, core: 2. Of those that a mesh axis runs over, the one named last changes fastest.
Arguments:
- activations: bfloat16 [4, 64, 8, 16, 128], P('batch', None, 'slab'), may hold values from -6 to 6
- grad_image: bfloat16 [4, 256, 256], P('batch', 'slab'), may hold values from -48 to 48
- pose_bin: int32 [4], P('batch'), may hold values from 0 to 31
- shift: int32 [4], P('batch'), may hold values from -8 to 8
- weight_a: bfloat16 [64, 2048], replicated, may hold values from -0.25 to 0.25
- bias_a: float32 [32], replicated, may hold values from -3 to 3
- weight_b: bfloat16 [32, 27], replicated, may hold values from -0.21875 to 0.21875
Outputs:
- grad_input: bfloat16 [4, 64, 8, 16, 128], P('batch', None, 'slab')
- grad_weight_a: float32 [64, 2048], replicated
- grad_bias_a: float32 [32], replicated
- grad_weight_b: float32 [32, 27], replicated
- grad_bias_b: float32 [1], replicated
The draws below stay inside these ranges and needn't reach their ends.
All inputs are finite; a program needn't handle non-finite values.
Results may differ from the reference program's by a relative error of at most 0.005.
Values may be sent and summed in bfloat16 or wider, within the bound.
A program may use at most 192 MiB of HBM per device.

```python
import math
import jax
import jax.numpy as jnp
from jax import lax

C0 = 64
C1 = 32
X = 256
U = 256
NBINS = 32
SMAX = 8
B = 4
YC = 16
XC = 128
NZC = 8


def plant(drawn, own_key, low, largest):
    index_at = [jax.random.randint(jax.random.fold_in(own_key, axis), (), 0, length) for axis, length in enumerate(drawn.shape)]
    longest = drawn.shape.index(max(drawn.shape))
    beside = index_at[:longest] + [(index_at[longest] + 1) % drawn.shape[longest]] + index_at[longest + 1:]
    return drawn.at[tuple(index_at)].set(low).at[tuple(beside)].set(largest)


def level_of(own_key, shape, pieces, smallest, top_value):
    def one(position, parts):
        steps = jax.random.uniform(jax.random.fold_in(jax.random.fold_in(own_key, 6), position), (parts,), jnp.float32, smallest / len(pieces), top_value / len(pieces))
        return jnp.repeat(jnp.exp(steps), shape[position] // parts).reshape((-1,) + (1,) * (len(shape) - position - 1))

    gain = one(*pieces[0])
    for cut in pieces[1:]:
        gain = gain * one(*cut)
    return gain


def centred(key, shape, spread, bound, pieces=(), held_as=jnp.bfloat16):
    gain = level_of(key, shape, pieces, -0.22, 0.18) if pieces else 1.0
    entries = jax.random.normal(key, shape, jnp.float32) * spread * gain
    return jnp.minimum(jnp.maximum(entries, -bound), bound).astype(held_as)


def setup_inputs(seed: int = 0) -> dict:
    key_list = jax.random.split(jax.random.key(seed), 8)
    activations = centred(key_list[0], (B, C0, NZC, YC, XC), 1.0, 6.0, ((0, 4), (2, 8)))
    grad_image = centred(key_list[1], (B, U, X), 8.0, 48.0, ((0, 4), (1, 8)))
    pose_bin = plant(jax.random.randint(key_list[2], (B,), 0, NBINS), jax.random.fold_in(key_list[2], 1), 0, NBINS - 1).astype(jnp.int32)
    shift = plant(jax.random.randint(key_list[3], (B,), 0 - SMAX, SMAX + 1), jax.random.fold_in(key_list[3], 1), 0 - SMAX, SMAX).astype(jnp.int32)
    weight_a = centred(key_list[4], (C0, 64 * C1), (8 * C0) ** -0.5, 0.25)
    bias_a = centred(key_list[5], (C1,), 0.5, 3.0, (), jnp.float32)
    weight_b = centred(key_list[6], (C1, 27), (27 * C1) ** -0.5, 0.21875)
    return dict(activations=activations, grad_image=grad_image, pose_bin=pose_bin, shift=shift, weight_a=weight_a, bias_a=bias_a, weight_b=weight_b)


forward_taps = (((0, 1), (-1, 3)), ((0, 2), (1, 0)))

def interp_weights(angle_bin, offset, plane_first, plane_count, row_count, total_depth, pixel_first, pixel_count, image_rows, bin_count):
    angle_value = (angle_bin.astype(jnp.float32) + 0.5) * (math.pi / bin_count)
    plane_pos = (plane_first + jnp.arange(plane_count, dtype=jnp.int32)).astype(jnp.float32)
    row_pos = jnp.arange(row_count, dtype=jnp.float32)
    center = (row_pos[None, :] - 0.5 * (row_count - 1)) * jnp.cos(angle_value) + (plane_pos[:, None] - 0.5 * (total_depth - 1)) * jnp.sin(angle_value) + (0.5 * (image_rows - 1) + offset.astype(jnp.float32))
    pixels = (pixel_first + jnp.arange(pixel_count, dtype=jnp.int32)).astype(jnp.float32)
    return jnp.maximum(1.0 - jnp.abs(pixels[None, :] - center.reshape(-1, 1)), 0.0)

def transposed_forward(padded_in, weight_a, bias_a, firsts, count, odd_first):
    chan_in = padded_in.shape[0]
    coarse_y = padded_in.shape[2] - 2
    coarse_x = padded_in.shape[3] - 2
    chan_out = bias_a.shape[0]
    parity_parts = []
    for par_z in range(2):
        row_parts = []
        for par_y in range(2):
            col_parts = []
            for par_x in range(2):
                running = jnp.zeros((chan_out, count * coarse_y * coarse_x), jnp.float32)
                for off_z, tap_z in forward_taps[par_z]:
                    for off_y, tap_y in forward_taps[par_y]:
                        for off_x, tap_x in forward_taps[par_x]:
                            start_z = firsts[par_z] + 1 + off_z
                            block = padded_in[:, start_z:start_z + count, 1 + off_y:1 + off_y + coarse_y, 1 + off_x:1 + off_x + coarse_x].reshape(chan_in, -1)
                            tap_index = tap_z * 16 + tap_y * 4 + tap_x
                            matrix = weight_a[:, tap_index * chan_out:(tap_index + 1) * chan_out]
                            running = running + jnp.dot(matrix.T, block, preferred_element_type=jnp.float32)
                col_parts.append(running.reshape(chan_out, count, coarse_y, coarse_x))
            row_parts.append(jnp.stack(col_parts, axis=-1))
        parity_parts.append(jnp.stack(row_parts, axis=3))
    if odd_first:
        ordered = [parity_parts[1], parity_parts[0]]
    else:
        ordered = [parity_parts[0], parity_parts[1]]
    joined = jnp.stack(ordered, axis=2).reshape(chan_out, 2 * count, 2 * coarse_y, 2 * coarse_x)
    return joined + bias_a[:, None, None, None]

def shifted_stack(padded_grad, planes, row_count, col_count):
    layers = []
    for tap_z in range(3):
        for tap_y in range(3):
            for tap_x in range(3):
                layers.append(padded_grad[tap_z:tap_z + planes, tap_y:tap_y + row_count, tap_x:tap_x + col_count].reshape(-1))
    return jnp.stack(layers)

def act_backward(pre_act, shifted, weight_b):
    gate_value = jax.nn.sigmoid(pre_act)
    act_value = pre_act * gate_value
    slope = gate_value * (1.0 + pre_act * (1.0 - gate_value))
    grad_raw = jnp.dot(weight_b.astype(jnp.float32), shifted, precision=lax.Precision.HIGHEST).reshape(pre_act.shape)
    return (act_value, slope * grad_raw)

def transposed_backward(extended, weight_a, act_in):
    chan_in, coarse_z, coarse_y, coarse_x = act_in.shape
    chan_out = extended.shape[0]
    split = extended.reshape(chan_out, coarse_z + 1, 2, coarse_y + 1, 2, coarse_x + 1, 2)
    split = split.transpose(0, 2, 4, 6, 1, 3, 5)
    blocks = []
    for tap_z in range(4):
        for tap_y in range(4):
            for tap_x in range(4):
                blocks.append(split[:, tap_z % 2, tap_y % 2, tap_x % 2, tap_z // 2:tap_z // 2 + coarse_z, tap_y // 2:tap_y // 2 + coarse_y, tap_x // 2:tap_x // 2 + coarse_x].reshape(chan_out, -1))
    stacked = jnp.concatenate(blocks, axis=0)
    grad_in = jnp.dot(weight_a, stacked, preferred_element_type=jnp.float32)
    grad_wa = lax.dot_general(act_in.reshape(chan_in, -1), stacked, (((1,), (1,)), ((), ())), preferred_element_type=jnp.float32)
    return (grad_in.reshape(act_in.shape).astype(jnp.bfloat16), grad_wa)

def reference(activations, grad_image, pose_bin, shift, weight_a, bias_a, weight_b):
    chan_out = bias_a.shape[0]

    def per_particle(packed):
        act_in, image_grad, angle_bin, offset = packed
        chan_in, coarse_z, coarse_y, coarse_x = act_in.shape
        total_depth, row_count, col_count = (2 * coarse_z, 2 * coarse_y, 2 * coarse_x)
        image_rows = image_grad.shape[0]
        weights = interp_weights(angle_bin, offset, 0, total_depth, row_count, total_depth, 0, image_rows, image_rows, NBINS)
        grad_volume = jnp.dot(weights, image_grad.astype(jnp.float32), precision=lax.Precision.HIGHEST).reshape(total_depth, row_count, col_count)
        padded_grad = jnp.pad(grad_volume, 1)
        shifted = shifted_stack(padded_grad, total_depth, row_count, col_count)
        padded_in = jnp.pad(act_in, ((0, 0), (1, 1), (1, 1), (1, 1)))
        pre_act = transposed_forward(padded_in, weight_a, bias_a, (0, 0), coarse_z, False)
        act_value, grad_raw = act_backward(pre_act, shifted, weight_b)
        grad_act = grad_raw.astype(jnp.bfloat16)
        extended = jnp.pad(grad_act, ((0, 0), (1, 1), (1, 1), (1, 1)))
        grad_in, grad_wa = transposed_backward(extended, weight_a, act_in)
        grad_ba = lax.optimization_barrier(jnp.sum(grad_act.astype(jnp.float32), axis=(1, 2, 3)))
        grad_wb = jnp.dot(act_value.reshape(chan_out, -1), shifted.T, precision=lax.Precision.HIGHEST)
        grad_bb = jnp.sum(grad_volume).reshape(1)
        return (grad_in, grad_wa, grad_ba, grad_wb, grad_bb)
    results = lax.map(per_particle, (activations, grad_image, pose_bin, shift))
    shape = activations.shape
    scale = 1.0 / math.sqrt(shape[0] * 2 * shape[2] * 2 * shape[3] * 2 * shape[4])
    return (results[0], lax.optimization_barrier(jnp.sum(results[1], axis=0)) * scale, lax.optimization_barrier(jnp.sum(results[2], axis=0)) * scale, lax.optimization_barrier(jnp.sum(results[3], axis=0)) * scale, lax.optimization_barrier(jnp.sum(results[4], axis=0)) * scale)
```

```python
import functools
import math

import jax
import jax.numpy as jnp
from jax import lax
from jax.experimental import pallas as pl
from jax.experimental.pallas import tpu as pltpu
from jax.sharding import PartitionSpec as P

NBINS = 32
MESH = pl.DeviceIdType.MESH
F32 = jnp.float32
BF16 = jnp.bfloat16
VMEM_LIMIT = 56 * 1024 * 1024


def nt_dot(a, b):
    return lax.dot_general(a, b, (((1,), (1,)), ((), ())), preferred_element_type=F32)


def mm(a, b):
    return jnp.dot(a, b, preferred_element_type=F32)


def gather_kernel(ns, x_ref, img_ref, halo_ref, all_ref, h_send, h_recv, g_send, g_recv):
    mb = lax.axis_index("batch")
    me = lax.axis_index("slab")
    barrier = pltpu.get_barrier_semaphore()
    for d in range(1, ns):
        pl.semaphore_signal(
            barrier, inc=1, device_id=(mb, lax.rem(me + d, ns)), device_id_type=MESH
        )
    pl.semaphore_wait(barrier, ns - 1)

    def to_right():
        return pltpu.make_async_remote_copy(
            src_ref=x_ref,
            dst_ref=halo_ref.at[0],
            send_sem=h_send.at[0],
            recv_sem=h_recv.at[0],
            device_id=(mb, lax.rem(me + 1, ns)),
            device_id_type=MESH,
        )

    def to_left():
        return pltpu.make_async_remote_copy(
            src_ref=x_ref,
            dst_ref=halo_ref.at[1],
            send_sem=h_send.at[1],
            recv_sem=h_recv.at[1],
            device_id=(mb, lax.rem(me + ns - 1, ns)),
            device_id_type=MESH,
        )

    @pl.when(me < ns - 1)
    def _():
        to_right().start()

    @pl.when(me > 0)
    def _():
        to_left().start()

    copies = []
    for d in range(1, ns):
        copy = pltpu.make_async_remote_copy(
            src_ref=img_ref,
            dst_ref=all_ref.at[me],
            send_sem=g_send.at[d - 1],
            recv_sem=g_recv.at[d - 1],
            device_id=(mb, lax.rem(me + d, ns)),
            device_id_type=MESH,
        )
        copy.start()
        copies.append(copy)
    all_ref[me] = img_ref[...]

    @pl.when(me == 0)
    def _():
        halo_ref[0] = jnp.zeros(halo_ref.shape[1:], halo_ref.dtype)

    @pl.when(me == ns - 1)
    def _():
        halo_ref[1] = jnp.zeros(halo_ref.shape[1:], halo_ref.dtype)

    for copy in copies:
        copy.wait()

    @pl.when(me < ns - 1)
    def _():
        to_right().wait_send()
        to_left().wait_recv()

    @pl.when(me > 0)
    def _():
        to_left().wait_send()
        to_right().wait_recv()


def local_kernel(
    ns,
    trig_ref,
    x_ref,
    halo_ref,
    img_ref,
    wa_ref,
    bias_ref,
    wbt_ref,
    gin_ref,
    gwa_ref,
    small_ref,
    tt_ref,
    g_ref,
    gt_ref,
    ga_ref,
    wf_ref,
    w4_ref,
    wb_ref,
    act_ref,
):
    me = lax.axis_index("slab")
    yc_n, c0, xc_n = x_ref.shape
    c1 = 32
    rows = img_ref.shape[0]
    depth = 2 * ns
    height = 2 * yc_n
    pos = yc_n * xc_n

    def iota(shape, dim):
        return lax.broadcasted_iota(jnp.int32, shape, dim)

    w = wa_ref[...]
    lane = iota((c0, 128), 1)
    for g in range(16):
        block = jnp.concatenate(
            [w[:, kz * 512 + g * 32 : kz * 512 + g * 32 + 32] for kz in range(4)], axis=1
        )
        w4_ref[:, g * 128 : (g + 1) * 128] = block
    zero_block = jnp.zeros((c0, 128), BF16)
    for py in range(2):
        for dyi in range(2):
            dy = py - 1 + dyi
            ky = py - 2 * dy + 1
            for dxi in range(3):
                dx = dxi - 1
                for px in range(2):
                    kx = px - 2 * dx + 1
                    for plane in range(3):
                        if 0 <= kx <= 3:
                            g = ky * 4 + kx
                            base = w4_ref[:, g * 128 : (g + 1) * 128]
                            half = jnp.zeros((c0, 64), BF16)
                            if plane == 0:
                                base = jnp.concatenate([base[:, 64:], half], axis=1)
                            elif plane == 2:
                                base = jnp.concatenate([half, base[:, :64]], axis=1)
                        else:
                            base = zero_block
                        wf_ref[
                            py, dyi, dxi, plane * c0 : (plane + 1) * c0, px * 128 : (px + 1) * 128
                        ] = base

    row = iota((96, 512), 0)
    col = iota((96, 512), 1)
    q = col >> 5
    tz, px_c, py_c = (q & 3, (q >> 2) & 1, (q >> 3) & 1)
    tx_r = (
        (row >= 24).astype(jnp.int32)
        + (row >= 48).astype(jnp.int32)
        + (row >= 72).astype(jnp.int32)
    )
    rem = row - 24 * tx_r
    az = (rem >> 2) - tz
    by = (rem & 3) - py_c
    cx = tx_r - px_c
    ok = (az >= 0) & (az < 3) & (by >= 0) & (by < 3) & (cx >= 0) & (cx < 3)
    index = jnp.where(ok, 9 * az + 3 * by + cx, -1)
    inside = ((tz > 0) | (me > 0)) & ((tz < 3) | (me < ns - 1))
    masked_index = jnp.where(inside, index, -1)
    wb_mat = jnp.zeros((96, 512), F32)
    for t in range(27):
        wb_mat = jnp.where(masked_index == t, wbt_ref[t : t + 1, :], wb_mat)
    wb_mat = wb_mat.astype(BF16)
    wb_ref[0:96, :] = wb_mat
    wb_ref[96:192, :] = wb_mat

    width = img_ref.shape[1]
    col_x = iota((width, 512), 1)
    fine = 2 * (col_x & 127) + (col_x >> 7) - 1
    sel = (iota((width, 512), 0) == fine).astype(F32).astype(BF16)
    ims = mm(img_ref[...], sel).astype(BF16)
    shape3 = (yc_n, 24, rows)
    j = iota(shape3, 1)
    y = 2 * iota(shape3, 0) + (j & 3) - 1
    z = 2 * me - 2 + (j >> 2)
    center = (
        (y.astype(F32) - 0.5 * (height - 1)) * trig_ref[0]
        + (z.astype(F32) - 0.5 * (depth - 1)) * trig_ref[1]
        + (0.5 * (rows - 1) + trig_ref[2])
    )
    interp = jnp.maximum(1.0 - jnp.abs(iota(shape3, 2).astype(F32) - center), 0.0)
    interp = jnp.where((y >= 0) & (y < height) & (z >= 0) & (z < depth), interp, 0.0)
    interp = interp.reshape(yc_n * 24, rows)
    hi = interp.astype(BF16)
    lo = (interp - hi.astype(F32)).astype(BF16)
    gtf = mm(hi, ims) + mm(lo, ims)
    eye = (iota((128, 128), 0) == iota((128, 128), 1)).astype(F32).astype(BF16)
    own_rows = iota((24, 256), 0)
    own = ((own_rows >> 2) >= 2) & ((own_rows >> 2) < 4) & ((own_rows & 3) > 0) & ((own_rows & 3) < 3)
    gb_total = jnp.zeros((24, 256), F32)
    sh_row = iota((384, 128), 0)
    shift_mat = (
        iota((384, 128), 1) == (sh_row & 127) + (sh_row >> 7) - 1
    ).astype(F32).astype(BF16)
    pad = jnp.zeros((128, 192), BF16)
    for dxi in range(3):
        tt_ref[dxi, 0:128, :] = pad
        tt_ref[dxi, pos + 128 : pos + 256, :] = pad
    for yc in range(yc_n):
        f = gtf[yc * 24 : (yc + 1) * 24]
        gb_total = gb_total + jnp.where(own, f[:, 128:384], 0.0)
        blk = jnp.concatenate([f[:, tx * 128 : (tx + 1) * 128] for tx in range(4)], axis=0)
        bhi = blk.astype(BF16)
        blo = (blk - bhi.astype(F32)).astype(BF16)
        gt = jnp.concatenate([bhi, blo], axis=0)
        gt_ref[yc] = gt
        g_ref[yc * 128 : (yc + 1) * 128, :] = nt_dot(eye, gt).astype(BF16)
        planes = jnp.concatenate([halo_ref[0, yc], x_ref[yc], halo_ref[1, yc]], axis=0)
        r = nt_dot(shift_mat, planes).astype(BF16)
        for dxi in range(3):
            tt_ref[dxi, (yc + 1) * 128 : (yc + 2) * 128, :] = r[dxi * 128 : (dxi + 1) * 128]

    zpad = jnp.zeros((128, 128), BF16)
    for kx in range(4):
        for py in range(2):
            ga_ref[kx, py, 0:128, :] = zpad
            ga_ref[kx, py, pos + 128 : pos + 256, :] = zpad
    step = 512
    xc_id = iota((step, 128), 0) & 127
    bias = bias_ref[...]

    def forward(it, sums):
        start = pl.multiple_of(it * step, step)
        new = []
        for py in range(2):
            pre = None
            for dyi in range(2):
                for dxi in range(3):
                    base = pl.multiple_of(start + (py + dyi) * 128, 128)
                    term = mm(tt_ref[dxi, pl.ds(base, step), :], wf_ref[py, dyi, dxi])
                    pre = term if pre is None else pre + term
            pre = pre + bias
            raw = mm(g_ref[pl.ds(start, step), :], wb_ref[:, py * 256 : (py + 1) * 256])
            gate = 0.5 * jnp.tanh(0.5 * pre) + 0.5
            act = pre * gate
            ga = (gate + act * (1.0 - gate)) * raw
            act_ref[pl.ds(start, step), py * 256 : (py + 1) * 256] = act.astype(BF16)
            new.append(sums[py] + jnp.sum(ga.reshape(step // 8, 8, 256), axis=0))
            dst = pl.ds(pl.multiple_of(start + 128, 128), step)
            g0, g1 = ga[:, :128], ga[:, 128:]
            ga_ref[1, py, dst, :] = g0.astype(BF16)
            ga_ref[2, py, dst, :] = g1.astype(BF16)
            ga_ref[0, py, dst, :] = jnp.where(xc_id == 0, 0.0, pltpu.roll(g1, 1, 0)).astype(BF16)
            ga_ref[3, py, dst, :] = jnp.where(
                xc_id == 127, 0.0, pltpu.roll(g0, step - 1, 0)
            ).astype(BF16)
        return tuple(new)

    zero_sum = jnp.zeros((8, 256), F32)
    sums = lax.fori_loop(0, pos // step, forward, (zero_sum, zero_sum))

    r_mat = jnp.zeros((192, 512), F32)
    for yc in range(yc_n):
        r_mat = r_mat + mm(gt_ref[yc], act_ref[yc * 128 : (yc + 1) * 128, :])
    r_sum = r_mat[0:96] + r_mat[96:192]
    mine = (tz > 0) & (tz < 3)
    own_index = jnp.where(mine, index, -1)
    lines = []
    for t in range(27):
        lines.append(jnp.sum(jnp.where(own_index == t, r_sum, 0.0), axis=0, keepdims=True))
    ba_row = jnp.sum(jnp.concatenate([sums[0], sums[1]], axis=1), axis=0, keepdims=True)
    lane5 = iota((1, 512), 1)
    tz5 = (lane5 >> 5) & 3
    lines.append(jnp.where((tz5 > 0) & (tz5 < 3), ba_row, 0.0))
    bb_total = jnp.sum(jnp.sum(gb_total, axis=0, keepdims=True), axis=1, keepdims=True)
    lines.append(jnp.where(lane5 == 0, bb_total, 0.0))
    lines.append(jnp.zeros((3, 512), F32))
    packed = jnp.concatenate(lines, axis=0)
    fold = packed[:, 0:128] + packed[:, 128:256] + packed[:, 256:384] + packed[:, 384:512]
    fold = fold + pltpu.roll(fold, 64, 1)
    fold = fold + pltpu.roll(fold, 32, 1)
    small_ref[...] = fold

    ky_src = ((1, 0), (0, 1), (1, 1), (0, 2))

    def patch(g, start, count):
        py, off = ky_src[g // 4]
        return ga_ref[g % 4, py, pl.ds(start + off * 128, count), :]

    def backward(it, carry):
        start = pl.multiple_of(it * step, step)
        total = None
        for pair in range(8):
            s = jnp.concatenate([patch(2 * pair, start, step), patch(2 * pair + 1, start, step)], axis=1)
            term = nt_dot(s, w4_ref[:, pair * 256 : (pair + 1) * 256])
            total = term if total is None else total + term
        total = total.astype(BF16)
        small_eye = eye[:c0, :c0]
        flipped = nt_dot(small_eye, total).astype(BF16)
        for k in range(step // 128):
            gin_ref[it * (step // 128) + k] = flipped[:, k * 128 : (k + 1) * 128]
        return carry

    lax.fori_loop(0, pos // step, backward, 0)
    xt = jnp.concatenate([x_ref[yc] for yc in range(yc_n)], axis=1)
    for pair in range(8):
        s = jnp.concatenate([patch(2 * pair, 0, pos), patch(2 * pair + 1, 0, pos)], axis=1)
        res = mm(xt, s).astype(BF16)
        gwa_ref[2 * pair] = res[:, :128]
        gwa_ref[2 * pair + 1] = res[:, 128:]


def reduce_kernel(
    nb, ns, scale, part_ref, small_ref, out_ref, osmall_ref,
    rb, mid, rs, full, srb, smid, srs, sems_b, sems_s, sems_g, sems_h, sems_x, sems_y,
):
    mb = lax.axis_index("batch")
    me = lax.axis_index("slab")
    barrier = pltpu.get_barrier_semaphore()
    for d in range(1, nb):
        pl.semaphore_signal(barrier, inc=1, device_id=(lax.rem(mb + d, nb), me), device_id_type=MESH)
    for d in range(1, ns):
        pl.semaphore_signal(barrier, inc=1, device_id=(mb, lax.rem(me + d, ns)), device_id_type=MESH)
    pl.semaphore_wait(barrier, nb + ns - 2)

    def send(src, dst, sems, d, device):
        copy = pltpu.make_async_remote_copy(
            src_ref=src,
            dst_ref=dst,
            send_sem=sems.at[0, d - 1],
            recv_sem=sems.at[1, d - 1],
            device_id=device,
            device_id_type=MESH,
        )
        copy.start()
        return copy

    first = []
    for d in range(1, nb):
        to = lax.rem(mb + d, nb)
        first.append(send(part_ref.at[to], rb.at[mb], sems_b, d, (to, me)))
        first.append(send(small_ref, srb.at[mb], sems_x, d, (to, me)))
    rb[mb] = part_ref[mb]
    srb[mb] = small_ref[...]
    for copy in first:
        copy.wait()
    acc = rb[0].astype(F32)
    sacc = srb[0]
    for b in range(1, nb):
        acc = acc + rb[b].astype(F32)
        sacc = sacc + srb[b]
    mid[...] = acc.astype(BF16)
    smid[...] = sacc
    second = []
    for d in range(1, ns):
        to = lax.rem(me + d, ns)
        second.append(send(mid.at[to], rs.at[me], sems_s, d, (mb, to)))
        second.append(send(smid, srs.at[me], sems_y, d, (mb, to)))
    rs[me] = mid[me]
    srs[me] = sacc
    for copy in second:
        copy.wait()
    acc = rs[0].astype(F32)
    sacc = srs[0]
    for s in range(1, ns):
        acc = acc + rs[s].astype(F32)
        sacc = sacc + srs[s]
    osmall_ref[...] = sacc * scale
    full[mb, me] = acc.astype(BF16)
    third = []
    for d in range(1, ns):
        to = lax.rem(me + d, ns)
        third.append(send(full.at[mb, me], full.at[mb, me], sems_g, d, (mb, to)))
    for copy in third:
        copy.wait()
    fourth = []
    for d in range(1, nb):
        to = lax.rem(mb + d, nb)
        fourth.append(send(full.at[mb], full.at[mb], sems_h, d, (to, me)))
    for copy in fourth:
        copy.wait()
    c0 = out_ref.shape[0]
    per = ns // 4
    for ky in range(4):
        groups = [
            full[ky, kx * per : (kx + 1) * per].astype(F32).reshape(c0, 128) * scale
            for kx in range(4)
        ]
        for kz in range(4):
            out_ref[:, kz * 512 + ky * 128 : kz * 512 + (ky + 1) * 128] = jnp.concatenate(
                [g[:, kz * 32 : (kz + 1) * 32] for g in groups], axis=1
            )


def body(nb, ns, activations, grad_image, pose_bin, shift, weight_a, bias_a, weight_b):
    vm = pl.BlockSpec(memory_space=pltpu.VMEM)
    _, c0, _, yc_n, xc_n = activations.shape
    c1 = bias_a.shape[0]
    pos = yc_n * xc_n
    x = activations[0, :, 0].transpose(1, 0, 2)
    img = grad_image[0]
    local_rows, width = img.shape
    halo, gathered = pl.pallas_call(
        functools.partial(gather_kernel, ns),
        out_shape=(
            jax.ShapeDtypeStruct((2,) + x.shape, BF16),
            jax.ShapeDtypeStruct((ns, local_rows, width), BF16),
        ),
        in_specs=[vm, vm],
        out_specs=(vm, vm),
        scratch_shapes=[
            pltpu.SemaphoreType.DMA((2,)),
            pltpu.SemaphoreType.DMA((2,)),
            pltpu.SemaphoreType.DMA((ns - 1,)),
            pltpu.SemaphoreType.DMA((ns - 1,)),
        ],
        compiler_params=pltpu.CompilerParams(
            collective_id=0, has_side_effects=True, vmem_limit_bytes=VMEM_LIMIT
        ),
        name="gather",
    )(x, img)
    angle = (pose_bin[0].astype(F32) + 0.5) * (math.pi / NBINS)
    trig = jnp.stack([jnp.cos(angle), jnp.sin(angle), shift[0].astype(F32)])
    bias_t = jnp.tile(bias_a, 8)[None]
    wbt = jnp.tile(weight_b.astype(F32).T, (1, 16))
    gin, gwa, small = pl.pallas_call(
        functools.partial(local_kernel, ns),
        out_shape=(
            jax.ShapeDtypeStruct((yc_n, c0, xc_n), BF16),
            jax.ShapeDtypeStruct((16, c0, 128), BF16),
            jax.ShapeDtypeStruct((32, 128), F32),
        ),
        in_specs=[pl.BlockSpec(memory_space=pltpu.SMEM)] + [vm] * 6,
        out_specs=(vm, vm, vm),
        scratch_shapes=[
            pltpu.VMEM((3, pos + 256, 192), BF16),
            pltpu.VMEM((pos, 192), BF16),
            pltpu.VMEM((yc_n, 192, 128), BF16),
            pltpu.VMEM((4, 2, pos + 256, 128), BF16),
            pltpu.VMEM((2, 2, 3, 192, 256), BF16),
            pltpu.VMEM((c0, 2048), BF16),
            pltpu.VMEM((192, 512), BF16),
            pltpu.VMEM((pos, 512), BF16),
        ],
        compiler_params=pltpu.CompilerParams(vmem_limit_bytes=VMEM_LIMIT),
        name="local",
    )(trig, x, halo, gathered.reshape(ns * local_rows, width), weight_a, bias_t, wbt)
    r = 256 // ns
    total_cells = nb * 2 * ns * 2 * yc_n * 2 * xc_n
    scale = 1.0 / math.sqrt(total_cells)
    grad_wa, osmall = pl.pallas_call(
        functools.partial(reduce_kernel, nb, ns, scale),
        out_shape=(
            jax.ShapeDtypeStruct(weight_a.shape, F32),
            jax.ShapeDtypeStruct((32, 128), F32),
        ),
        in_specs=[vm, vm],
        out_specs=(vm, vm),
        scratch_shapes=[
            pltpu.VMEM((nb, ns, r, 128), BF16),
            pltpu.VMEM((ns, r, 128), BF16),
            pltpu.VMEM((ns, r, 128), BF16),
            pltpu.VMEM((nb, ns, r, 128), BF16),
            pltpu.VMEM((nb, 32, 128), F32),
            pltpu.VMEM((32, 128), F32),
            pltpu.VMEM((ns, 32, 128), F32),
            pltpu.SemaphoreType.DMA((2, nb - 1)),
            pltpu.SemaphoreType.DMA((2, ns - 1)),
            pltpu.SemaphoreType.DMA((2, ns - 1)),
            pltpu.SemaphoreType.DMA((2, nb - 1)),
            pltpu.SemaphoreType.DMA((2, nb - 1)),
            pltpu.SemaphoreType.DMA((2, ns - 1)),
        ],
        compiler_params=pltpu.CompilerParams(
            collective_id=1, has_side_effects=True, vmem_limit_bytes=VMEM_LIMIT
        ),
        name="reduce",
    )(gwa.reshape(nb, ns, r, 128), small)
    grad_in = gin.transpose(1, 0, 2)[None, :, None]
    return (grad_in, grad_wa, osmall[27, :c1], osmall[:27, :c1].T, osmall[28, :1])


def solution(mesh):
    return jax.shard_map(
        functools.partial(body, mesh.shape["batch"], mesh.shape["slab"]),
        mesh=mesh,
        in_specs=(
            P("batch", None, "slab", None, None),
            P("batch", "slab", None),
            P("batch"),
            P("batch"),
            P(),
            P(),
            P(),
        ),
        out_specs=(P("batch", None, "slab", None, None), P(), P(), P(), P()),
        check_vma=False,
    )
```

```python
import functools
import math

import jax
import jax.numpy as jnp
from jax import lax
from jax.experimental import pallas as pl
from jax.experimental.pallas import tpu as pltpu
from jax.sharding import PartitionSpec as P

NBINS = 32
MESH = pl.DeviceIdType.MESH
F32 = jnp.float32
BF16 = jnp.bfloat16
VMEM_LIMIT = 56 * 1024 * 1024


def nt_dot(a, b):
    return lax.dot_general(a, b, (((1,), (1,)), ((), ())), preferred_element_type=F32)


def mm(a, b):
    return jnp.dot(a, b, preferred_element_type=F32)


def gather_kernel(ns, x_ref, img_ref, halo_ref, all_ref, h_send, h_recv, g_send, g_recv):
    mb = lax.axis_index("batch")
    me = lax.axis_index("slab")
    barrier = pltpu.get_barrier_semaphore()
    for d in range(1, ns):
        pl.semaphore_signal(
            barrier, inc=1, device_id=(mb, lax.rem(me + d, ns)), device_id_type=MESH
        )
    pl.semaphore_wait(barrier, ns - 1)

    def to_right():
        return pltpu.make_async_remote_copy(
            src_ref=x_ref,
            dst_ref=halo_ref.at[0],
            send_sem=h_send.at[0],
            recv_sem=h_recv.at[0],
            device_id=(mb, lax.rem(me + 1, ns)),
            device_id_type=MESH,
        )

    def to_left():
        return pltpu.make_async_remote_copy(
            src_ref=x_ref,
            dst_ref=halo_ref.at[1],
            send_sem=h_send.at[1],
            recv_sem=h_recv.at[1],
            device_id=(mb, lax.rem(me + ns - 1, ns)),
            device_id_type=MESH,
        )

    @pl.when(me < ns - 1)
    def _():
        to_right().start()

    @pl.when(me > 0)
    def _():
        to_left().start()

    copies = []
    for d in range(1, ns):
        copy = pltpu.make_async_remote_copy(
            src_ref=img_ref,
            dst_ref=all_ref.at[me],
            send_sem=g_send.at[d - 1],
            recv_sem=g_recv.at[d - 1],
            device_id=(mb, lax.rem(me + d, ns)),
            device_id_type=MESH,
        )
        copy.start()
        copies.append(copy)
    all_ref[me] = img_ref[...]

    @pl.when(me == 0)
    def _():
        halo_ref[0] = jnp.zeros(halo_ref.shape[1:], halo_ref.dtype)

    @pl.when(me == ns - 1)
    def _():
        halo_ref[1] = jnp.zeros(halo_ref.shape[1:], halo_ref.dtype)

    for copy in copies:
        copy.wait()

    @pl.when(me < ns - 1)
    def _():
        to_right().wait_send()
        to_left().wait_recv()

    @pl.when(me > 0)
    def _():
        to_left().wait_send()
        to_right().wait_recv()


def local_kernel(
    ns,
    trig_ref,
    x_ref,
    halo_ref,
    img_ref,
    wa_ref,
    bias_ref,
    taps_ref,
    gin_ref,
    gwa_ref,
    small_ref,
    tt_ref,
    g_ref,
    gt_ref,
    ga_ref,
    wf_ref,
    w4_ref,
    wb_ref,
    act_ref,
):
    me = lax.axis_index("slab")
    yc_n, c0, xc_n = x_ref.shape
    c1 = 32
    rows = img_ref.shape[0]
    depth = 2 * ns
    height = 2 * yc_n
    pos = yc_n * xc_n

    def iota(shape, dim):
        return lax.broadcasted_iota(jnp.int32, shape, dim)

    w = wa_ref[...]
    lane = iota((c0, 128), 1)
    for g in range(16):
        block = jnp.concatenate(
            [w[:, kz * 512 + g * 32 : kz * 512 + g * 32 + 32] for kz in range(4)], axis=1
        )
        w4_ref[:, g * 128 : (g + 1) * 128] = block
    zero_block = jnp.zeros((c0, 128), BF16)
    for py in range(2):
        for dyi in range(2):
            dy = py - 1 + dyi
            ky = py - 2 * dy + 1
            for dxi in range(3):
                dx = dxi - 1
                for px in range(2):
                    kx = px - 2 * dx + 1
                    for plane in range(3):
                        if 0 <= kx <= 3:
                            g = ky * 4 + kx
                            base = w4_ref[:, g * 128 : (g + 1) * 128]
                            half = jnp.zeros((c0, 64), BF16)
                            if plane == 0:
                                base = jnp.concatenate([base[:, 64:], half], axis=1)
                            elif plane == 2:
                                base = jnp.concatenate([half, base[:, :64]], axis=1)
                        else:
                            base = zero_block
                        wf_ref[
                            py, dyi, dxi, plane * c0 : (plane + 1) * c0, px * 128 : (px + 1) * 128
                        ] = base

    row = iota((96, 512), 0)
    col = iota((96, 512), 1)
    q = col >> 5
    tz, px_c, py_c = (q & 3, (q >> 2) & 1, (q >> 3) & 1)
    tx_r = (
        (row >= 24).astype(jnp.int32)
        + (row >= 48).astype(jnp.int32)
        + (row >= 72).astype(jnp.int32)
    )
    rem = row - 24 * tx_r
    az = (rem >> 2) - tz
    by = (rem & 3) - py_c
    cx = tx_r - px_c
    ok = (az >= 0) & (az < 3) & (by >= 0) & (by < 3) & (cx >= 0) & (cx < 3)
    index = jnp.where(ok, 9 * az + 3 * by + cx, -1)
    inside = ((tz > 0) | (me > 0)) & ((tz < 3) | (me < ns - 1))
    masked_index = jnp.where(inside, index, -1)
    spread = (iota((c1, 512), 0) == (iota((c1, 512), 1) & 31)).astype(F32).astype(BF16)
    eye_t = (iota((27, 27), 0) == iota((27, 27), 1)).astype(F32).astype(BF16)
    wbt = mm(nt_dot(eye_t, taps_ref[...]).astype(BF16), spread)
    wb_mat = jnp.zeros((96, 512), F32)
    for t in range(27):
        wb_mat = jnp.where(masked_index == t, wbt[t : t + 1, :], wb_mat)
    wb_mat = wb_mat.astype(BF16)
    wb_ref[0:96, :] = wb_mat
    wb_ref[96:192, :] = wb_mat

    width = img_ref.shape[1]
    col_x = iota((width, 512), 1)
    fine = 2 * (col_x & 127) + (col_x >> 7) - 1
    sel = (iota((width, 512), 0) == fine).astype(F32).astype(BF16)
    ims = mm(img_ref[...], sel).astype(BF16)
    shape3 = (yc_n, 24, rows)
    j = iota(shape3, 1)
    y = 2 * iota(shape3, 0) + (j & 3) - 1
    z = 2 * me - 2 + (j >> 2)
    center = (
        (y.astype(F32) - 0.5 * (height - 1)) * trig_ref[0]
        + (z.astype(F32) - 0.5 * (depth - 1)) * trig_ref[1]
        + (0.5 * (rows - 1) + trig_ref[2])
    )
    interp = jnp.maximum(1.0 - jnp.abs(iota(shape3, 2).astype(F32) - center), 0.0)
    interp = jnp.where((y >= 0) & (y < height) & (z >= 0) & (z < depth), interp, 0.0)
    interp = interp.reshape(yc_n * 24, rows)
    hi = interp.astype(BF16)
    lo = (interp - hi.astype(F32)).astype(BF16)
    gtf = mm(hi, ims) + mm(lo, ims)
    eye = (iota((128, 128), 0) == iota((128, 128), 1)).astype(F32).astype(BF16)
    own_rows = iota((24, 256), 0)
    own = ((own_rows >> 2) >= 2) & ((own_rows >> 2) < 4) & ((own_rows & 3) > 0) & ((own_rows & 3) < 3)
    gb_total = jnp.zeros((24, 256), F32)
    sh_row = iota((384, 128), 0)
    shift_mat = (
        iota((384, 128), 1) == (sh_row & 127) + (sh_row >> 7) - 1
    ).astype(F32).astype(BF16)
    pad = jnp.zeros((128, 192), BF16)
    for dxi in range(3):
        tt_ref[dxi, 0:128, :] = pad
        tt_ref[dxi, pos + 128 : pos + 256, :] = pad
    for yc in range(yc_n):
        f = gtf[yc * 24 : (yc + 1) * 24]
        gb_total = gb_total + jnp.where(own, f[:, 128:384], 0.0)
        blk = jnp.concatenate([f[:, tx * 128 : (tx + 1) * 128] for tx in range(4)], axis=0)
        bhi = blk.astype(BF16)
        blo = (blk - bhi.astype(F32)).astype(BF16)
        gt = jnp.concatenate([bhi, blo], axis=0)
        gt_ref[yc] = gt
        g_ref[yc * 128 : (yc + 1) * 128, :] = nt_dot(eye, gt).astype(BF16)
        planes = jnp.concatenate([halo_ref[0, yc], x_ref[yc], halo_ref[1, yc]], axis=0)
        r = nt_dot(shift_mat, planes).astype(BF16)
        for dxi in range(3):
            tt_ref[dxi, (yc + 1) * 128 : (yc + 2) * 128, :] = r[dxi * 128 : (dxi + 1) * 128]

    zpad = jnp.zeros((128, 128), BF16)
    for kx in range(4):
        for py in range(2):
            ga_ref[kx, py, 0:128, :] = zpad
            ga_ref[kx, py, pos + 128 : pos + 256, :] = zpad
    step = 512
    xc_id = iota((step, 128), 0) & 127
    bias = jnp.concatenate([bias_ref[...]] * 8, axis=1)

    def forward(it, sums):
        start = pl.multiple_of(it * step, step)
        new = []
        for py in range(2):
            pre = None
            for dyi in range(2):
                for dxi in range(3):
                    base = pl.multiple_of(start + (py + dyi) * 128, 128)
                    term = mm(tt_ref[dxi, pl.ds(base, step), :], wf_ref[py, dyi, dxi])
                    pre = term if pre is None else pre + term
            pre = pre + bias
            raw = mm(g_ref[pl.ds(start, step), :], wb_ref[:, py * 256 : (py + 1) * 256])
            gate = 0.5 * jnp.tanh(0.5 * pre) + 0.5
            act = pre * gate
            ga = (gate + act * (1.0 - gate)) * raw
            act_ref[pl.ds(start, step), py * 256 : (py + 1) * 256] = act.astype(BF16)
            new.append(sums[py] + jnp.sum(ga.reshape(step // 8, 8, 256), axis=0))
            dst = pl.ds(pl.multiple_of(start + 128, 128), step)
            g0, g1 = ga[:, :128], ga[:, 128:]
            ga_ref[1, py, dst, :] = g0.astype(BF16)
            ga_ref[2, py, dst, :] = g1.astype(BF16)
            ga_ref[0, py, dst, :] = jnp.where(xc_id == 0, 0.0, pltpu.roll(g1, 1, 0)).astype(BF16)
            ga_ref[3, py, dst, :] = jnp.where(
                xc_id == 127, 0.0, pltpu.roll(g0, step - 1, 0)
            ).astype(BF16)
        return tuple(new)

    zero_sum = jnp.zeros((8, 256), F32)
    sums = lax.fori_loop(0, pos // step, forward, (zero_sum, zero_sum))

    r_mat = jnp.zeros((192, 512), F32)
    for yc in range(yc_n):
        r_mat = r_mat + mm(gt_ref[yc], act_ref[yc * 128 : (yc + 1) * 128, :])
    r_sum = r_mat[0:96] + r_mat[96:192]
    mine = (tz > 0) & (tz < 3)
    own_index = jnp.where(mine, index, -1)
    lines = []
    for t in range(27):
        lines.append(jnp.sum(jnp.where(own_index == t, r_sum, 0.0), axis=0, keepdims=True))
    ba_row = jnp.sum(jnp.concatenate([sums[0], sums[1]], axis=1), axis=0, keepdims=True)
    lane5 = iota((1, 512), 1)
    tz5 = (lane5 >> 5) & 3
    lines.append(jnp.where((tz5 > 0) & (tz5 < 3), ba_row, 0.0))
    bb_total = jnp.sum(jnp.sum(gb_total, axis=0, keepdims=True), axis=1, keepdims=True)
    lines.append(jnp.where(lane5 == 0, bb_total, 0.0))
    lines.append(jnp.zeros((3, 512), F32))
    packed = jnp.concatenate(lines, axis=0)
    fold = packed[:, 0:128] + packed[:, 128:256] + packed[:, 256:384] + packed[:, 384:512]
    fold = fold + pltpu.roll(fold, 64, 1)
    fold = fold + pltpu.roll(fold, 32, 1)
    group = iota((8, 128), 1) >> 5
    tight = fold[0:8]
    for k in range(1, 4):
        tight = jnp.where(group == k, fold[8 * k : 8 * k + 8], tight)
    small_ref[...] = tight

    ky_src = ((1, 0), (0, 1), (1, 1), (0, 2))

    def patch(g, start, count):
        py, off = ky_src[g // 4]
        return ga_ref[g % 4, py, pl.ds(start + off * 128, count), :]

    def backward(it, carry):
        start = pl.multiple_of(it * step, step)
        total = None
        for pair in range(8):
            s = jnp.concatenate([patch(2 * pair, start, step), patch(2 * pair + 1, start, step)], axis=1)
            term = nt_dot(s, w4_ref[:, pair * 256 : (pair + 1) * 256])
            total = term if total is None else total + term
        total = total.astype(BF16)
        small_eye = eye[:c0, :c0]
        flipped = nt_dot(small_eye, total).astype(BF16)
        for k in range(step // 128):
            gin_ref[it * (step // 128) + k] = flipped[:, k * 128 : (k + 1) * 128]
        return carry

    lax.fori_loop(0, pos // step, backward, 0)
    xt = jnp.concatenate([x_ref[yc] for yc in range(yc_n)], axis=1)
    for pair in range(8):
        s = jnp.concatenate([patch(2 * pair, 0, pos), patch(2 * pair + 1, 0, pos)], axis=1)
        res = mm(xt, s).astype(BF16)
        gwa_ref[2 * pair] = res[:, :128]
        gwa_ref[2 * pair + 1] = res[:, 128:]


def reduce_kernel(
    nb, ns, part_ref, small_ref, full, osmall_ref,
    rb, mid, rs, srb, smid, srs, sems_b, sems_s, sems_g, sems_h, sems_x, sems_y,
):
    mb = lax.axis_index("batch")
    me = lax.axis_index("slab")
    barrier = pltpu.get_barrier_semaphore()
    for d in range(1, nb):
        pl.semaphore_signal(barrier, inc=1, device_id=(lax.rem(mb + d, nb), me), device_id_type=MESH)
    for d in range(1, ns):
        pl.semaphore_signal(barrier, inc=1, device_id=(mb, lax.rem(me + d, ns)), device_id_type=MESH)
    pl.semaphore_wait(barrier, nb + ns - 2)

    def send(src, dst, sems, d, device):
        copy = pltpu.make_async_remote_copy(
            src_ref=src,
            dst_ref=dst,
            send_sem=sems.at[0, d - 1],
            recv_sem=sems.at[1, d - 1],
            device_id=device,
            device_id_type=MESH,
        )
        copy.start()
        return copy

    first = []
    for d in range(1, nb):
        to = lax.rem(mb + d, nb)
        first.append(send(part_ref.at[to], rb.at[mb], sems_b, d, (to, me)))
        first.append(send(small_ref, srb.at[mb], sems_x, d, (to, me)))
    rb[mb] = part_ref[mb]
    srb[mb] = small_ref[...]
    for copy in first:
        copy.wait()
    acc = rb[0].astype(F32)
    sacc = srb[0]
    for b in range(1, nb):
        acc = acc + rb[b].astype(F32)
        sacc = sacc + srb[b]
    mid[...] = acc.astype(BF16)
    smid[...] = sacc
    second = []
    for d in range(1, ns):
        to = lax.rem(me + d, ns)
        second.append(send(mid.at[to], rs.at[me], sems_s, d, (mb, to)))
        second.append(send(smid, srs.at[me], sems_y, d, (mb, to)))
    rs[me] = mid[me]
    srs[me] = sacc
    for copy in second:
        copy.wait()
    acc = rs[0].astype(F32)
    sacc = srs[0]
    for s in range(1, ns):
        acc = acc + rs[s].astype(F32)
        sacc = sacc + srs[s]
    osmall_ref[...] = sacc
    full[mb, me] = acc.astype(BF16)
    third = []
    for d in range(1, ns):
        to = lax.rem(me + d, ns)
        third.append(send(full.at[mb, me], full.at[mb, me], sems_g, d, (mb, to)))
    for copy in third:
        copy.wait()
    fourth = []
    for d in range(1, nb):
        to = lax.rem(mb + d, nb)
        fourth.append(send(full.at[mb], full.at[mb], sems_h, d, (to, me)))
    for copy in fourth:
        copy.wait()


def finish_kernel(scale, full_ref, osmall_ref, out_ref, ba_ref, wb_ref, bb_ref):
    c0 = out_ref.shape[0]
    per = full_ref.shape[1] // 4
    for ky in range(4):
        groups = [
            full_ref[ky, kx * per : (kx + 1) * per].astype(F32).reshape(c0, 128) * scale
            for kx in range(4)
        ]
        for kz in range(4):
            out_ref[:, kz * 512 + ky * 128 : kz * 512 + (ky + 1) * 128] = jnp.concatenate(
                [g[:, kz * 32 : (kz + 1) * 32] for g in groups], axis=1
            )
    tight = osmall_ref[...] * scale
    table = jnp.concatenate([tight[:, k * 32 : (k + 1) * 32] for k in range(4)], axis=0)
    eye = (
        lax.broadcasted_iota(jnp.int32, (32, 32), 0) == lax.broadcasted_iota(jnp.int32, (32, 32), 1)
    ).astype(F32)
    flipped = lax.dot_general(
        eye, table, (((1,), (1,)), ((), ())), precision=lax.Precision.HIGHEST,
        preferred_element_type=F32,
    )
    wb_ref[...] = flipped[:, 0:27]
    ba_ref[...] = table[27:28, :]
    bb_ref[...] = table[28:29, 0:1]


def body(nb, ns, activations, grad_image, pose_bin, shift, weight_a, bias_a, weight_b):
    vm = pl.BlockSpec(memory_space=pltpu.VMEM)
    _, c0, _, yc_n, xc_n = activations.shape
    c1 = bias_a.shape[0]
    pos = yc_n * xc_n
    x = activations[0, :, 0].transpose(1, 0, 2)
    img = grad_image[0]
    local_rows, width = img.shape
    halo, gathered = pl.pallas_call(
        functools.partial(gather_kernel, ns),
        out_shape=(
            jax.ShapeDtypeStruct((2,) + x.shape, BF16),
            jax.ShapeDtypeStruct((ns, local_rows, width), BF16),
        ),
        in_specs=[vm, vm],
        out_specs=(vm, vm),
        scratch_shapes=[
            pltpu.SemaphoreType.DMA((2,)),
            pltpu.SemaphoreType.DMA((2,)),
            pltpu.SemaphoreType.DMA((ns - 1,)),
            pltpu.SemaphoreType.DMA((ns - 1,)),
        ],
        compiler_params=pltpu.CompilerParams(
            collective_id=0, has_side_effects=True, vmem_limit_bytes=VMEM_LIMIT
        ),
        name="gather",
    )(x, img)
    angle = (pose_bin[0].astype(F32) + 0.5) * (math.pi / NBINS)
    trig = jnp.stack([jnp.cos(angle), jnp.sin(angle), shift[0].astype(F32)])
    gin, gwa, small = pl.pallas_call(
        functools.partial(local_kernel, ns),
        out_shape=(
            jax.ShapeDtypeStruct((yc_n, c0, xc_n), BF16),
            jax.ShapeDtypeStruct((16, c0, 128), BF16),
            jax.ShapeDtypeStruct((8, 128), F32),
        ),
        in_specs=[pl.BlockSpec(memory_space=pltpu.SMEM)] + [vm] * 6,
        out_specs=(vm, vm, vm),
        scratch_shapes=[
            pltpu.VMEM((3, pos + 256, 192), BF16),
            pltpu.VMEM((pos, 192), BF16),
            pltpu.VMEM((yc_n, 192, 128), BF16),
            pltpu.VMEM((4, 2, pos + 256, 128), BF16),
            pltpu.VMEM((2, 2, 3, 192, 256), BF16),
            pltpu.VMEM((c0, 2048), BF16),
            pltpu.VMEM((192, 512), BF16),
            pltpu.VMEM((pos, 512), BF16),
        ],
        compiler_params=pltpu.CompilerParams(vmem_limit_bytes=VMEM_LIMIT),
        name="local",
    )(trig, x, halo, gathered.reshape(ns * local_rows, width), weight_a, bias_a.reshape(1, c1), weight_b)
    r = 256 // ns
    total_cells = nb * 2 * ns * 2 * yc_n * 2 * xc_n
    scale = 1.0 / math.sqrt(total_cells)
    full, osmall = pl.pallas_call(
        functools.partial(reduce_kernel, nb, ns),
        out_shape=(
            jax.ShapeDtypeStruct((nb, ns, r, 128), BF16),
            jax.ShapeDtypeStruct((8, 128), F32),
        ),
        in_specs=[vm, vm],
        out_specs=(vm, vm),
        scratch_shapes=[
            pltpu.VMEM((nb, ns, r, 128), BF16),
            pltpu.VMEM((ns, r, 128), BF16),
            pltpu.VMEM((ns, r, 128), BF16),
            pltpu.VMEM((nb, 8, 128), F32),
            pltpu.VMEM((8, 128), F32),
            pltpu.VMEM((ns, 8, 128), F32),
            pltpu.SemaphoreType.DMA((2, nb - 1)),
            pltpu.SemaphoreType.DMA((2, ns - 1)),
            pltpu.SemaphoreType.DMA((2, ns - 1)),
            pltpu.SemaphoreType.DMA((2, nb - 1)),
            pltpu.SemaphoreType.DMA((2, nb - 1)),
            pltpu.SemaphoreType.DMA((2, ns - 1)),
        ],
        compiler_params=pltpu.CompilerParams(
            collective_id=1, has_side_effects=True, vmem_limit_bytes=VMEM_LIMIT
        ),
        name="reduce",
    )(gwa.reshape(nb, ns, r, 128), small)
    grad_in = gin.transpose(1, 0, 2)[None, :, None]
    grad_wa, grad_ba, grad_wb, grad_bb = pl.pallas_call(
        functools.partial(finish_kernel, scale),
        out_shape=(
            jax.ShapeDtypeStruct(weight_a.shape, F32),
            jax.ShapeDtypeStruct((1, c1), F32),
            jax.ShapeDtypeStruct(weight_b.shape, F32),
            jax.ShapeDtypeStruct((1, 1), F32),
        ),
        in_specs=[vm, vm],
        out_specs=(vm, vm, vm, vm),
        compiler_params=pltpu.CompilerParams(vmem_limit_bytes=VMEM_LIMIT),
        name="finish",
    )(full, osmall)
    return (grad_in, grad_wa, grad_ba.reshape(c1), grad_wb, grad_bb.reshape(1))


def solution(mesh):
    return jax.shard_map(
        functools.partial(body, mesh.shape["batch"], mesh.shape["slab"]),
        mesh=mesh,
        in_specs=(
            P("batch", None, "slab", None, None),
            P("batch", "slab", None),
            P("batch"),
            P("batch"),
            P(),
            P(),
            P(),
        ),
        out_specs=(P("batch", None, "slab", None, None), P(), P(), P(), P()),
        check_vma=False,
    )
```

```python
import functools
import math

import jax
import jax.numpy as jnp
from jax import lax
from jax.experimental import pallas as pl
from jax.experimental.pallas import tpu as pltpu
from jax.sharding import PartitionSpec as P

NBINS = 32
MESH = pl.DeviceIdType.MESH
F32 = jnp.float32
BF16 = jnp.bfloat16
VMEM_LIMIT = 56 * 1024 * 1024


def nt_dot(a, b):
    return lax.dot_general(a, b, (((1,), (1,)), ((), ())), preferred_element_type=F32)


def mm(a, b):
    return jnp.dot(a, b, preferred_element_type=F32)


def gather_kernel(ns, x_ref, img_ref, halo_ref, all_ref, h_send, h_recv, g_send, g_recv):
    mb = lax.axis_index("batch")
    me = lax.axis_index("slab")
    barrier = pltpu.get_barrier_semaphore()
    for d in range(1, ns):
        pl.semaphore_signal(
            barrier, inc=1, device_id=(mb, lax.rem(me + d, ns)), device_id_type=MESH
        )
    pl.semaphore_wait(barrier, ns - 1)

    def to_right():
        return pltpu.make_async_remote_copy(
            src_ref=x_ref,
            dst_ref=halo_ref.at[0],
            send_sem=h_send.at[0],
            recv_sem=h_recv.at[0],
            device_id=(mb, lax.rem(me + 1, ns)),
            device_id_type=MESH,
        )

    def to_left():
        return pltpu.make_async_remote_copy(
            src_ref=x_ref,
            dst_ref=halo_ref.at[1],
            send_sem=h_send.at[1],
            recv_sem=h_recv.at[1],
            device_id=(mb, lax.rem(me + ns - 1, ns)),
            device_id_type=MESH,
        )

    @pl.when(me < ns - 1)
    def _():
        to_right().start()

    @pl.when(me > 0)
    def _():
        to_left().start()

    copies = []
    for d in range(1, ns):
        copy = pltpu.make_async_remote_copy(
            src_ref=img_ref,
            dst_ref=all_ref.at[me],
            send_sem=g_send.at[d - 1],
            recv_sem=g_recv.at[d - 1],
            device_id=(mb, lax.rem(me + d, ns)),
            device_id_type=MESH,
        )
        copy.start()
        copies.append(copy)
    all_ref[me] = img_ref[...]

    @pl.when(me == 0)
    def _():
        halo_ref[0] = jnp.zeros(halo_ref.shape[1:], halo_ref.dtype)

    @pl.when(me == ns - 1)
    def _():
        halo_ref[1] = jnp.zeros(halo_ref.shape[1:], halo_ref.dtype)

    for copy in copies:
        copy.wait()

    @pl.when(me < ns - 1)
    def _():
        to_right().wait_send()
        to_left().wait_recv()

    @pl.when(me > 0)
    def _():
        to_left().wait_send()
        to_right().wait_recv()


def local_kernel(
    nb,
    ns,
    trig_ref,
    x_ref,
    halo_ref,
    img_ref,
    wa_ref,
    bias_ref,
    taps_ref,
    gin_ref,
    full,
    osmall_ref,
    tt_ref,
    g_ref,
    gt_ref,
    ga_ref,
    wf_ref,
    w4_ref,
    wb_ref,
    act_ref,
    part,
    r0,
    m0,
    rb,
    mid,
    rs,
    sr0,
    sm0,
    srb,
    smid,
    srs,
    sems_c,
    sems_b,
    sems_z,
    sems_gz,
    sems_gb,
    sems_gc,
    sems_sc,
    sems_sb,
    sems_sz,
):
    mb = lax.axis_index("batch")
    me = lax.axis_index("slab")
    nh = ns // 2
    core = lax.rem(me, 2)
    hs = me // 2
    partner = (mb, me + 1 - 2 * core)
    barrier = pltpu.get_barrier_semaphore()
    pl.semaphore_signal(barrier, inc=1, device_id=partner, device_id_type=MESH)
    for d in range(1, nb):
        pl.semaphore_signal(barrier, inc=1, device_id=(lax.rem(mb + d, nb), me), device_id_type=MESH)
    for d in range(1, nh):
        peer = (mb, 2 * lax.rem(hs + d, nh) + core)
        pl.semaphore_signal(barrier, inc=1, device_id=peer, device_id_type=MESH)

    def send(src, dst, sems, d, device):
        copy = pltpu.make_async_remote_copy(
            src_ref=src,
            dst_ref=dst,
            send_sem=sems.at[0, d - 1],
            recv_sem=sems.at[1, d - 1],
            device_id=device,
            device_id_type=MESH,
        )
        copy.start()
        return copy

    yc_n, c0, xc_n = x_ref.shape
    c1 = 32
    rows = img_ref.shape[0]
    depth = 2 * ns
    height = 2 * yc_n
    pos = yc_n * xc_n

    def iota(shape, dim):
        return lax.broadcasted_iota(jnp.int32, shape, dim)

    w = wa_ref[...]
    lane = iota((c0, 128), 1)
    for g in range(16):
        block = jnp.concatenate(
            [w[:, kz * 512 + g * 32 : kz * 512 + g * 32 + 32] for kz in range(4)], axis=1
        )
        w4_ref[:, g * 128 : (g + 1) * 128] = block
    zero_block = jnp.zeros((c0, 128), BF16)
    for py in range(2):
        for dyi in range(2):
            dy = py - 1 + dyi
            ky = py - 2 * dy + 1
            for dxi in range(3):
                dx = dxi - 1
                for px in range(2):
                    kx = px - 2 * dx + 1
                    for plane in range(3):
                        if 0 <= kx <= 3:
                            g = ky * 4 + kx
                            base = w4_ref[:, g * 128 : (g + 1) * 128]
                            half = jnp.zeros((c0, 64), BF16)
                            if plane == 0:
                                base = jnp.concatenate([base[:, 64:], half], axis=1)
                            elif plane == 2:
                                base = jnp.concatenate([half, base[:, :64]], axis=1)
                        else:
                            base = zero_block
                        wf_ref[
                            py, dyi, dxi, plane * c0 : (plane + 1) * c0, px * 128 : (px + 1) * 128
                        ] = base

    row = iota((96, 512), 0)
    col = iota((96, 512), 1)
    q = col >> 5
    tz, px_c, py_c = (q & 3, (q >> 2) & 1, (q >> 3) & 1)
    tx_r = (
        (row >= 24).astype(jnp.int32)
        + (row >= 48).astype(jnp.int32)
        + (row >= 72).astype(jnp.int32)
    )
    rem = row - 24 * tx_r
    az = (rem >> 2) - tz
    by = (rem & 3) - py_c
    cx = tx_r - px_c
    ok = (az >= 0) & (az < 3) & (by >= 0) & (by < 3) & (cx >= 0) & (cx < 3)
    index = jnp.where(ok, 9 * az + 3 * by + cx, -1)
    inside = ((tz > 0) | (me > 0)) & ((tz < 3) | (me < ns - 1))
    masked_index = jnp.where(inside, index, -1)
    spread = (iota((c1, 512), 0) == (iota((c1, 512), 1) & 31)).astype(F32).astype(BF16)
    eye_t = (iota((27, 27), 0) == iota((27, 27), 1)).astype(F32).astype(BF16)
    wbt = mm(nt_dot(eye_t, taps_ref[...]).astype(BF16), spread)
    wb_mat = jnp.zeros((96, 512), F32)
    for t in range(27):
        wb_mat = jnp.where(masked_index == t, wbt[t : t + 1, :], wb_mat)
    wb_mat = wb_mat.astype(BF16)
    wb_ref[0:96, :] = wb_mat
    wb_ref[96:192, :] = wb_mat

    width = img_ref.shape[1]
    col_x = iota((width, 512), 1)
    fine = 2 * (col_x & 127) + (col_x >> 7) - 1
    sel = (iota((width, 512), 0) == fine).astype(F32).astype(BF16)
    ims = mm(img_ref[...], sel).astype(BF16)
    shape3 = (yc_n, 24, rows)
    j = iota(shape3, 1)
    y = 2 * iota(shape3, 0) + (j & 3) - 1
    z = 2 * me - 2 + (j >> 2)
    center = (
        (y.astype(F32) - 0.5 * (height - 1)) * trig_ref[0]
        + (z.astype(F32) - 0.5 * (depth - 1)) * trig_ref[1]
        + (0.5 * (rows - 1) + trig_ref[2])
    )
    interp = jnp.maximum(1.0 - jnp.abs(iota(shape3, 2).astype(F32) - center), 0.0)
    interp = jnp.where((y >= 0) & (y < height) & (z >= 0) & (z < depth), interp, 0.0)
    interp = interp.reshape(yc_n * 24, rows)
    hi = interp.astype(BF16)
    lo = (interp - hi.astype(F32)).astype(BF16)
    gtf = mm(hi, ims) + mm(lo, ims)
    eye = (iota((128, 128), 0) == iota((128, 128), 1)).astype(F32).astype(BF16)
    own_rows = iota((24, 256), 0)
    own = ((own_rows >> 2) >= 2) & ((own_rows >> 2) < 4) & ((own_rows & 3) > 0) & ((own_rows & 3) < 3)
    gb_total = jnp.zeros((24, 256), F32)
    sh_row = iota((384, 128), 0)
    shift_mat = (
        iota((384, 128), 1) == (sh_row & 127) + (sh_row >> 7) - 1
    ).astype(F32).astype(BF16)
    pad = jnp.zeros((128, 192), BF16)
    for dxi in range(3):
        tt_ref[dxi, 0:128, :] = pad
        tt_ref[dxi, pos + 128 : pos + 256, :] = pad
    for yc in range(yc_n):
        f = gtf[yc * 24 : (yc + 1) * 24]
        gb_total = gb_total + jnp.where(own, f[:, 128:384], 0.0)
        blk = jnp.concatenate([f[:, tx * 128 : (tx + 1) * 128] for tx in range(4)], axis=0)
        bhi = blk.astype(BF16)
        blo = (blk - bhi.astype(F32)).astype(BF16)
        gt = jnp.concatenate([bhi, blo], axis=0)
        gt_ref[yc] = gt
        g_ref[yc * 128 : (yc + 1) * 128, :] = nt_dot(eye, gt).astype(BF16)
        planes = jnp.concatenate([halo_ref[0, yc], x_ref[yc], halo_ref[1, yc]], axis=0)
        r = nt_dot(shift_mat, planes).astype(BF16)
        for dxi in range(3):
            tt_ref[dxi, (yc + 1) * 128 : (yc + 2) * 128, :] = r[dxi * 128 : (dxi + 1) * 128]

    zpad = jnp.zeros((128, 128), BF16)
    for kx in range(4):
        for py in range(2):
            ga_ref[kx, py, 0:128, :] = zpad
            ga_ref[kx, py, pos + 128 : pos + 256, :] = zpad
    step = 512
    xc_id = iota((step, 128), 0) & 127
    bias = jnp.concatenate([bias_ref[...]] * 8, axis=1)

    def forward(it, sums):
        start = pl.multiple_of(it * step, step)
        new = []
        for py in range(2):
            pre = None
            for dyi in range(2):
                for dxi in range(3):
                    base = pl.multiple_of(start + (py + dyi) * 128, 128)
                    term = mm(tt_ref[dxi, pl.ds(base, step), :], wf_ref[py, dyi, dxi])
                    pre = term if pre is None else pre + term
            pre = pre + bias
            raw = mm(g_ref[pl.ds(start, step), :], wb_ref[:, py * 256 : (py + 1) * 256])
            gate = 0.5 * jnp.tanh(0.5 * pre) + 0.5
            act = pre * gate
            ga = (gate + act * (1.0 - gate)) * raw
            act_ref[pl.ds(start, step), py * 256 : (py + 1) * 256] = act.astype(BF16)
            new.append(sums[py] + jnp.sum(ga.reshape(step // 8, 8, 256), axis=0))
            dst = pl.ds(pl.multiple_of(start + 128, 128), step)
            g0, g1 = ga[:, :128], ga[:, 128:]
            ga_ref[1, py, dst, :] = g0.astype(BF16)
            ga_ref[2, py, dst, :] = g1.astype(BF16)
            ga_ref[0, py, dst, :] = jnp.where(xc_id == 0, 0.0, pltpu.roll(g1, 1, 0)).astype(BF16)
            ga_ref[3, py, dst, :] = jnp.where(
                xc_id == 127, 0.0, pltpu.roll(g0, step - 1, 0)
            ).astype(BF16)
        return tuple(new)

    zero_sum = jnp.zeros((8, 256), F32)
    sums = lax.fori_loop(0, pos // step, forward, (zero_sum, zero_sum))

    r_mat = jnp.zeros((192, 512), F32)
    for yc in range(yc_n):
        r_mat = r_mat + mm(gt_ref[yc], act_ref[yc * 128 : (yc + 1) * 128, :])
    r_sum = r_mat[0:96] + r_mat[96:192]
    mine = (tz > 0) & (tz < 3)
    own_index = jnp.where(mine, index, -1)
    lines = []
    for t in range(27):
        lines.append(jnp.sum(jnp.where(own_index == t, r_sum, 0.0), axis=0, keepdims=True))
    ba_row = jnp.sum(jnp.concatenate([sums[0], sums[1]], axis=1), axis=0, keepdims=True)
    lane5 = iota((1, 512), 1)
    tz5 = (lane5 >> 5) & 3
    lines.append(jnp.where((tz5 > 0) & (tz5 < 3), ba_row, 0.0))
    bb_total = jnp.sum(jnp.sum(gb_total, axis=0, keepdims=True), axis=1, keepdims=True)
    lines.append(jnp.where(lane5 == 0, bb_total, 0.0))
    lines.append(jnp.zeros((3, 512), F32))
    packed = jnp.concatenate(lines, axis=0)
    fold = packed[:, 0:128] + packed[:, 128:256] + packed[:, 256:384] + packed[:, 384:512]
    fold = fold + pltpu.roll(fold, 64, 1)
    fold = fold + pltpu.roll(fold, 32, 1)
    group = iota((8, 128), 1) >> 5
    tight = fold[0:8]
    for k in range(1, 4):
        tight = jnp.where(group == k, fold[8 * k : 8 * k + 8], tight)
    sr0[core] = tight

    ky_src = ((1, 0), (0, 1), (1, 1), (0, 2))

    def patch(g, start, count):
        py, off = ky_src[g // 4]
        return ga_ref[g % 4, py, pl.ds(start + off * 128, count), :]

    def backward(it, carry):
        start = pl.multiple_of(it * step, step)
        total = None
        for pair in range(8):
            s = jnp.concatenate([patch(2 * pair, start, step), patch(2 * pair + 1, start, step)], axis=1)
            term = nt_dot(s, w4_ref[:, pair * 256 : (pair + 1) * 256])
            total = term if total is None else total + term
        total = total.astype(BF16)
        small_eye = eye[:c0, :c0]
        flipped = nt_dot(small_eye, total).astype(BF16)
        for k in range(step // 128):
            gin_ref[it * (step // 128) + k] = flipped[:, k * 128 : (k + 1) * 128]
        return carry

    xt = jnp.concatenate([x_ref[yc] for yc in range(yc_n)], axis=1)
    per, r = part.shape[2] // 2, part.shape[3]
    for pair in range(8):
        s = jnp.concatenate([patch(2 * pair, 0, pos), patch(2 * pair + 1, 0, pos)], axis=1)
        res = mm(xt, s)
        for h in range(2):
            part[pair // 4, pair % 4, h * per : (h + 1) * per] = (
                res[:, h * 128 : (h + 1) * 128].reshape(per, r, 128).astype(BF16)
            )

    pl.semaphore_wait(barrier, nb + nh - 1)
    pair_copies = [
        send(part.at[1 - core], r0, sems_c, 1, partner),
        send(sr0.at[core], sr0.at[core], sems_sc, 1, partner),
    ]
    half = pos // step // 4
    lax.fori_loop(0, half, backward, 0)
    for copy in pair_copies:
        copy.wait()
    m0[...] = (part[core].astype(F32) + r0[...].astype(F32)).astype(BF16)
    sm0[...] = sr0[0] + sr0[1]
    first = []
    for d in range(1, nb):
        to = lax.rem(mb + d, nb)
        first.append(send(m0.at[to], rb.at[mb], sems_b, d, (to, me)))
        first.append(send(sm0, srb.at[mb], sems_sb, d, (to, me)))
    rb[mb] = m0[mb]
    srb[mb] = sm0[...]
    lax.fori_loop(half, pos // step, backward, 0)
    for copy in first:
        copy.wait()
    acc = rb[0].astype(F32)
    sacc = srb[0]
    for b in range(1, nb):
        acc = acc + rb[b].astype(F32)
        sacc = sacc + srb[b]
    mid[...] = acc.astype(BF16)
    smid[...] = sacc
    second = []
    for d in range(1, nh):
        to = lax.rem(hs + d, nh)
        second.append(send(mid.at[to], rs.at[hs], sems_z, d, (mb, 2 * to + core)))
        second.append(send(smid, srs.at[hs], sems_sz, d, (mb, 2 * to + core)))
    rs[hs] = mid[hs]
    srs[hs] = sacc
    for copy in second:
        copy.wait()
    acc = rs[0].astype(F32)
    sacc = srs[0]
    for k in range(1, nh):
        acc = acc + rs[k].astype(F32)
        sacc = sacc + srs[k]
    osmall_ref[...] = sacc
    full[core, mb, hs] = acc.astype(BF16)
    third = []
    for d in range(1, nh):
        to = (mb, 2 * lax.rem(hs + d, nh) + core)
        third.append(send(full.at[core, mb, hs], full.at[core, mb, hs], sems_gz, d, to))
    for copy in third:
        copy.wait()
    fourth = []
    for d in range(1, nb):
        to = (lax.rem(mb + d, nb), me)
        fourth.append(send(full.at[core, mb], full.at[core, mb], sems_gb, d, to))
    for copy in fourth:
        copy.wait()
    send(full.at[core], full.at[core], sems_gc, 1, partner).wait()


def finish_kernel(scale, full_ref, osmall_ref, out_ref, ba_ref, wb_ref, bb_ref):
    c0 = out_ref.shape[0]
    per = full_ref.shape[2] // 2
    for ky in range(4):
        groups = [
            full_ref[ky // 2, 2 * (ky % 2) + kx // 2, (kx % 2) * per : (kx % 2 + 1) * per]
            .astype(F32)
            .reshape(c0, 128)
            * scale
            for kx in range(4)
        ]
        for kz in range(4):
            out_ref[:, kz * 512 + ky * 128 : kz * 512 + (ky + 1) * 128] = jnp.concatenate(
                [g[:, kz * 32 : (kz + 1) * 32] for g in groups], axis=1
            )
    tight = osmall_ref[...] * scale
    table = jnp.concatenate([tight[:, k * 32 : (k + 1) * 32] for k in range(4)], axis=0)
    eye = (
        lax.broadcasted_iota(jnp.int32, (32, 32), 0) == lax.broadcasted_iota(jnp.int32, (32, 32), 1)
    ).astype(F32)
    flipped = lax.dot_general(
        eye, table, (((1,), (1,)), ((), ())), precision=lax.Precision.HIGHEST,
        preferred_element_type=F32,
    )
    wb_ref[...] = flipped[:, 0:27]
    ba_ref[...] = table[27:28, :]
    bb_ref[...] = table[28:29, 0:1]


def body(nb, ns, activations, grad_image, pose_bin, shift, weight_a, bias_a, weight_b):
    vm = pl.BlockSpec(memory_space=pltpu.VMEM)
    _, c0, _, yc_n, xc_n = activations.shape
    c1 = bias_a.shape[0]
    pos = yc_n * xc_n
    x = activations[0, :, 0].transpose(1, 0, 2)
    img = grad_image[0]
    local_rows, width = img.shape
    halo, gathered = pl.pallas_call(
        functools.partial(gather_kernel, ns),
        out_shape=(
            jax.ShapeDtypeStruct((2,) + x.shape, BF16),
            jax.ShapeDtypeStruct((ns, local_rows, width), BF16),
        ),
        in_specs=[vm, vm],
        out_specs=(vm, vm),
        scratch_shapes=[
            pltpu.SemaphoreType.DMA((2,)),
            pltpu.SemaphoreType.DMA((2,)),
            pltpu.SemaphoreType.DMA((ns - 1,)),
            pltpu.SemaphoreType.DMA((ns - 1,)),
        ],
        compiler_params=pltpu.CompilerParams(
            collective_id=0, has_side_effects=True, vmem_limit_bytes=VMEM_LIMIT
        ),
        name="gather",
    )(x, img)
    angle = (pose_bin[0].astype(F32) + 0.5) * (math.pi / NBINS)
    trig = jnp.stack([jnp.cos(angle), jnp.sin(angle), shift[0].astype(F32)])
    nh = ns // 2
    r = 512 // (nb * nh)
    total_cells = nb * 2 * ns * 2 * yc_n * 2 * xc_n
    scale = 1.0 / math.sqrt(total_cells)
    gin, full, osmall = pl.pallas_call(
        functools.partial(local_kernel, nb, ns),
        out_shape=(
            jax.ShapeDtypeStruct((yc_n, c0, xc_n), BF16),
            jax.ShapeDtypeStruct((2, nb, nh, r, 128), BF16),
            jax.ShapeDtypeStruct((8, 128), F32),
        ),
        in_specs=[pl.BlockSpec(memory_space=pltpu.SMEM)] + [vm] * 6,
        out_specs=(vm, vm, vm),
        scratch_shapes=[
            pltpu.VMEM((3, pos + 256, 192), BF16),
            pltpu.VMEM((pos, 192), BF16),
            pltpu.VMEM((yc_n, 192, 128), BF16),
            pltpu.VMEM((4, 2, pos + 256, 128), BF16),
            pltpu.VMEM((2, 2, 3, 192, 256), BF16),
            pltpu.VMEM((c0, 2048), BF16),
            pltpu.VMEM((192, 512), BF16),
            pltpu.VMEM((pos, 512), BF16),
            pltpu.VMEM((2, nb, nh, r, 128), BF16),
            pltpu.VMEM((nb, nh, r, 128), BF16),
            pltpu.VMEM((nb, nh, r, 128), BF16),
            pltpu.VMEM((nb, nh, r, 128), BF16),
            pltpu.VMEM((nh, r, 128), BF16),
            pltpu.VMEM((nh, r, 128), BF16),
            pltpu.VMEM((2, 8, 128), F32),
            pltpu.VMEM((8, 128), F32),
            pltpu.VMEM((nb, 8, 128), F32),
            pltpu.VMEM((8, 128), F32),
            pltpu.VMEM((nh, 8, 128), F32),
            pltpu.SemaphoreType.DMA((2, 1)),
            pltpu.SemaphoreType.DMA((2, nb - 1)),
            pltpu.SemaphoreType.DMA((2, nh - 1)),
            pltpu.SemaphoreType.DMA((2, nh - 1)),
            pltpu.SemaphoreType.DMA((2, nb - 1)),
            pltpu.SemaphoreType.DMA((2, 1)),
            pltpu.SemaphoreType.DMA((2, 1)),
            pltpu.SemaphoreType.DMA((2, nb - 1)),
            pltpu.SemaphoreType.DMA((2, nh - 1)),
        ],
        compiler_params=pltpu.CompilerParams(
            collective_id=1, has_side_effects=True, vmem_limit_bytes=VMEM_LIMIT
        ),
        name="local",
    )(
        trig, x, halo, gathered.reshape(ns * local_rows, width), weight_a,
        bias_a.reshape(1, c1), weight_b,
    )
    grad_in = gin.transpose(1, 0, 2)[None, :, None]
    grad_wa, grad_ba, grad_wb, grad_bb = pl.pallas_call(
        functools.partial(finish_kernel, scale),
        out_shape=(
            jax.ShapeDtypeStruct(weight_a.shape, F32),
            jax.ShapeDtypeStruct((1, c1), F32),
            jax.ShapeDtypeStruct(weight_b.shape, F32),
            jax.ShapeDtypeStruct((1, 1), F32),
        ),
        in_specs=[vm, vm],
        out_specs=(vm, vm, vm, vm),
        compiler_params=pltpu.CompilerParams(vmem_limit_bytes=VMEM_LIMIT),
        name="finish",
    )(full, osmall)
    return (grad_in, grad_wa, grad_ba.reshape(c1), grad_wb, grad_bb.reshape(1))


def solution(mesh):
    return jax.shard_map(
        functools.partial(body, mesh.shape["batch"], mesh.shape["slab"]),
        mesh=mesh,
        in_specs=(
            P("batch", None, "slab", None, None),
            P("batch", "slab", None),
            P("batch"),
            P("batch"),
            P(),
            P(),
            P(),
        ),
        out_specs=(P("batch", None, "slab", None, None), P(), P(), P(), P()),
        check_vma=False,
    )
```

```python
import functools
import math

import jax
import jax.numpy as jnp
from jax import lax
from jax.experimental import pallas as pl
from jax.experimental.pallas import tpu as pltpu
from jax.sharding import PartitionSpec as P

NBINS = 32
MESH = pl.DeviceIdType.MESH
F32 = jnp.float32
BF16 = jnp.bfloat16
VMEM_LIMIT = 56 * 1024 * 1024


def nt_dot(a, b):
    return lax.dot_general(a, b, (((1,), (1,)), ((), ())), preferred_element_type=F32)


def mm(a, b):
    return jnp.dot(a, b, preferred_element_type=F32)


def local_kernel(
    nb,
    ns,
    trig_ref,
    x_ref,
    img_ref,
    wa_ref,
    bias_ref,
    taps_ref,
    gin_ref,
    full,
    osmall_ref,
    tt_ref,
    g_ref,
    gt_ref,
    ga_ref,
    wf_ref,
    w4_ref,
    wb_ref,
    act_ref,
    halo_ref,
    all_ref,
    h_send,
    h_recv,
    g_send,
    g_recv,
    part,
    r0,
    m0,
    rb,
    mid,
    rs,
    sr0,
    sm0,
    srb,
    smid,
    srs,
    sems_c,
    sems_b,
    sems_z,
    sems_gz,
    sems_gb,
    sems_gc,
    sems_sc,
    sems_sb,
    sems_sz,
):
    mb = lax.axis_index("batch")
    me = lax.axis_index("slab")
    nh = ns // 2
    core = lax.rem(me, 2)
    hs = me // 2
    partner = (mb, me + 1 - 2 * core)
    barrier = pltpu.get_barrier_semaphore()
    for d in range(1, nb):
        pl.semaphore_signal(barrier, inc=1, device_id=(lax.rem(mb + d, nb), me), device_id_type=MESH)
    for d in range(1, ns):
        peer = (mb, lax.rem(me + d, ns))
        pl.semaphore_signal(barrier, inc=1, device_id=peer, device_id_type=MESH)
    pl.semaphore_wait(barrier, nb + ns - 2)

    images = []
    for d in range(1, ns):
        copy = pltpu.make_async_remote_copy(
            src_ref=img_ref,
            dst_ref=all_ref.at[me],
            send_sem=g_send.at[d - 1],
            recv_sem=g_recv.at[d - 1],
            device_id=(mb, lax.rem(me + d, ns)),
            device_id_type=MESH,
        )
        copy.start()
        images.append(copy)

    def to_right():
        return pltpu.make_async_remote_copy(
            src_ref=x_ref,
            dst_ref=halo_ref.at[0],
            send_sem=h_send.at[0],
            recv_sem=h_recv.at[0],
            device_id=(mb, lax.rem(me + 1, ns)),
            device_id_type=MESH,
        )

    def to_left():
        return pltpu.make_async_remote_copy(
            src_ref=x_ref,
            dst_ref=halo_ref.at[1],
            send_sem=h_send.at[1],
            recv_sem=h_recv.at[1],
            device_id=(mb, lax.rem(me + ns - 1, ns)),
            device_id_type=MESH,
        )

    @pl.when(me < ns - 1)
    def _():
        to_right().start()

    @pl.when(me > 0)
    def _():
        to_left().start()

    all_ref[me] = img_ref[...]

    @pl.when(me == 0)
    def _():
        halo_ref[0] = jnp.zeros(halo_ref.shape[1:], halo_ref.dtype)

    @pl.when(me == ns - 1)
    def _():
        halo_ref[1] = jnp.zeros(halo_ref.shape[1:], halo_ref.dtype)

    def send(src, dst, sems, d, device):
        copy = pltpu.make_async_remote_copy(
            src_ref=src,
            dst_ref=dst,
            send_sem=sems.at[0, d - 1],
            recv_sem=sems.at[1, d - 1],
            device_id=device,
            device_id_type=MESH,
        )
        copy.start()
        return copy

    yc_n, c0, xc_n = x_ref.shape
    c1 = 32
    rows = ns * img_ref.shape[0]
    depth = 2 * ns
    height = 2 * yc_n
    pos = yc_n * xc_n

    def iota(shape, dim):
        return lax.broadcasted_iota(jnp.int32, shape, dim)

    w = wa_ref[...]
    lane = iota((c0, 128), 1)
    for g in range(16):
        block = jnp.concatenate(
            [w[:, kz * 512 + g * 32 : kz * 512 + g * 32 + 32] for kz in range(4)], axis=1
        )
        w4_ref[:, g * 128 : (g + 1) * 128] = block
    zero_block = jnp.zeros((c0, 128), BF16)
    for py in range(2):
        for dyi in range(2):
            dy = py - 1 + dyi
            ky = py - 2 * dy + 1
            for dxi in range(3):
                dx = dxi - 1
                for px in range(2):
                    kx = px - 2 * dx + 1
                    for plane in range(3):
                        if 0 <= kx <= 3:
                            g = ky * 4 + kx
                            base = w4_ref[:, g * 128 : (g + 1) * 128]
                            half = jnp.zeros((c0, 64), BF16)
                            if plane == 0:
                                base = jnp.concatenate([base[:, 64:], half], axis=1)
                            elif plane == 2:
                                base = jnp.concatenate([half, base[:, :64]], axis=1)
                        else:
                            base = zero_block
                        wf_ref[
                            py, dyi, dxi, plane * c0 : (plane + 1) * c0, px * 128 : (px + 1) * 128
                        ] = base

    row = iota((96, 512), 0)
    col = iota((96, 512), 1)
    q = col >> 5
    tz, px_c, py_c = (q & 3, (q >> 2) & 1, (q >> 3) & 1)
    tx_r = (
        (row >= 24).astype(jnp.int32)
        + (row >= 48).astype(jnp.int32)
        + (row >= 72).astype(jnp.int32)
    )
    rem = row - 24 * tx_r
    az = (rem >> 2) - tz
    by = (rem & 3) - py_c
    cx = tx_r - px_c
    ok = (az >= 0) & (az < 3) & (by >= 0) & (by < 3) & (cx >= 0) & (cx < 3)
    index = jnp.where(ok, 9 * az + 3 * by + cx, -1)
    inside = ((tz > 0) | (me > 0)) & ((tz < 3) | (me < ns - 1))
    masked_index = jnp.where(inside, index, -1)
    spread = (iota((c1, 512), 0) == (iota((c1, 512), 1) & 31)).astype(F32).astype(BF16)
    eye_t = (iota((27, 27), 0) == iota((27, 27), 1)).astype(F32).astype(BF16)
    wbt = mm(nt_dot(eye_t, taps_ref[...]).astype(BF16), spread)
    wb_mat = jnp.zeros((96, 512), F32)
    for t in range(27):
        wb_mat = jnp.where(masked_index == t, wbt[t : t + 1, :], wb_mat)
    wb_mat = wb_mat.astype(BF16)
    wb_ref[0:96, :] = wb_mat
    wb_ref[96:192, :] = wb_mat

    width = img_ref.shape[1]
    col_x = iota((width, 512), 1)
    fine = 2 * (col_x & 127) + (col_x >> 7) - 1
    sel = (iota((width, 512), 0) == fine).astype(F32).astype(BF16)
    for copy in images:
        copy.wait()
    whole_image = all_ref[...].astype(F32).reshape(rows, width).astype(BF16)
    ims = mm(whole_image, sel).astype(BF16)
    shape3 = (yc_n, 24, rows)
    j = iota(shape3, 1)
    y = 2 * iota(shape3, 0) + (j & 3) - 1
    z = 2 * me - 2 + (j >> 2)
    center = (
        (y.astype(F32) - 0.5 * (height - 1)) * trig_ref[0]
        + (z.astype(F32) - 0.5 * (depth - 1)) * trig_ref[1]
        + (0.5 * (rows - 1) + trig_ref[2])
    )
    interp = jnp.maximum(1.0 - jnp.abs(iota(shape3, 2).astype(F32) - center), 0.0)
    interp = jnp.where((y >= 0) & (y < height) & (z >= 0) & (z < depth), interp, 0.0)
    interp = interp.reshape(yc_n * 24, rows)
    hi = interp.astype(BF16)
    lo = (interp - hi.astype(F32)).astype(BF16)
    gtf = mm(hi, ims) + mm(lo, ims)
    eye = (iota((128, 128), 0) == iota((128, 128), 1)).astype(F32).astype(BF16)
    own_rows = iota((24, 256), 0)
    own = ((own_rows >> 2) >= 2) & ((own_rows >> 2) < 4) & ((own_rows & 3) > 0) & ((own_rows & 3) < 3)
    gb_total = jnp.zeros((24, 256), F32)
    sh_row = iota((384, 128), 0)
    shift_mat = (
        iota((384, 128), 1) == (sh_row & 127) + (sh_row >> 7) - 1
    ).astype(F32).astype(BF16)
    pad = jnp.zeros((128, 192), BF16)
    for dxi in range(3):
        tt_ref[dxi, 0:128, :] = pad
        tt_ref[dxi, pos + 128 : pos + 256, :] = pad
    for yc in range(yc_n):
        f = gtf[yc * 24 : (yc + 1) * 24]
        gb_total = gb_total + jnp.where(own, f[:, 128:384], 0.0)
        blk = jnp.concatenate([f[:, tx * 128 : (tx + 1) * 128] for tx in range(4)], axis=0)
        bhi = blk.astype(BF16)
        blo = (blk - bhi.astype(F32)).astype(BF16)
        gt = jnp.concatenate([bhi, blo], axis=0)
        gt_ref[yc] = gt
        g_ref[yc * 128 : (yc + 1) * 128, :] = nt_dot(eye, gt).astype(BF16)

    @pl.when(me < ns - 1)
    def _():
        to_right().wait_send()
        to_left().wait_recv()

    @pl.when(me > 0)
    def _():
        to_left().wait_send()
        to_right().wait_recv()

    for yc in range(yc_n):
        planes = jnp.concatenate([halo_ref[0, yc], x_ref[yc], halo_ref[1, yc]], axis=0)
        r = nt_dot(shift_mat, planes).astype(BF16)
        for dxi in range(3):
            tt_ref[dxi, (yc + 1) * 128 : (yc + 2) * 128, :] = r[dxi * 128 : (dxi + 1) * 128]

    zpad = jnp.zeros((128, 128), BF16)
    for kx in range(4):
        for py in range(2):
            ga_ref[kx, py, 0:128, :] = zpad
            ga_ref[kx, py, pos + 128 : pos + 256, :] = zpad
    step = 512
    xc_id = iota((step, 128), 0) & 127
    bias = jnp.concatenate([bias_ref[...]] * 8, axis=1)

    def forward(it, sums):
        start = pl.multiple_of(it * step, step)
        new = []
        for py in range(2):
            pre = None
            for dyi in range(2):
                for dxi in range(3):
                    base = pl.multiple_of(start + (py + dyi) * 128, 128)
                    term = mm(tt_ref[dxi, pl.ds(base, step), :], wf_ref[py, dyi, dxi])
                    pre = term if pre is None else pre + term
            pre = pre + bias
            raw = mm(g_ref[pl.ds(start, step), :], wb_ref[:, py * 256 : (py + 1) * 256])
            gate = 0.5 * jnp.tanh(0.5 * pre) + 0.5
            act = pre * gate
            ga = (gate + act * (1.0 - gate)) * raw
            act_ref[pl.ds(start, step), py * 256 : (py + 1) * 256] = act.astype(BF16)
            new.append(sums[py] + jnp.sum(ga.reshape(step // 8, 8, 256), axis=0))
            dst = pl.ds(pl.multiple_of(start + 128, 128), step)
            g0, g1 = ga[:, :128], ga[:, 128:]
            ga_ref[1, py, dst, :] = g0.astype(BF16)
            ga_ref[2, py, dst, :] = g1.astype(BF16)
            ga_ref[0, py, dst, :] = jnp.where(xc_id == 0, 0.0, pltpu.roll(g1, 1, 0)).astype(BF16)
            ga_ref[3, py, dst, :] = jnp.where(
                xc_id == 127, 0.0, pltpu.roll(g0, step - 1, 0)
            ).astype(BF16)
        return tuple(new)

    zero_sum = jnp.zeros((8, 256), F32)
    sums = lax.fori_loop(0, pos // step, forward, (zero_sum, zero_sum))

    r_mat = jnp.zeros((192, 512), F32)
    for yc in range(yc_n):
        r_mat = r_mat + mm(gt_ref[yc], act_ref[yc * 128 : (yc + 1) * 128, :])
    r_sum = r_mat[0:96] + r_mat[96:192]
    mine = (tz > 0) & (tz < 3)
    own_index = jnp.where(mine, index, -1)
    lines = []
    for t in range(27):
        lines.append(jnp.sum(jnp.where(own_index == t, r_sum, 0.0), axis=0, keepdims=True))
    ba_row = jnp.sum(jnp.concatenate([sums[0], sums[1]], axis=1), axis=0, keepdims=True)
    lane5 = iota((1, 512), 1)
    tz5 = (lane5 >> 5) & 3
    lines.append(jnp.where((tz5 > 0) & (tz5 < 3), ba_row, 0.0))
    bb_total = jnp.sum(jnp.sum(gb_total, axis=0, keepdims=True), axis=1, keepdims=True)
    lines.append(jnp.where(lane5 == 0, bb_total, 0.0))
    lines.append(jnp.zeros((3, 512), F32))
    packed = jnp.concatenate(lines, axis=0)
    fold = packed[:, 0:128] + packed[:, 128:256] + packed[:, 256:384] + packed[:, 384:512]
    fold = fold + pltpu.roll(fold, 64, 1)
    fold = fold + pltpu.roll(fold, 32, 1)
    group = iota((8, 128), 1) >> 5
    tight = fold[0:8]
    for k in range(1, 4):
        tight = jnp.where(group == k, fold[8 * k : 8 * k + 8], tight)
    sr0[core] = tight

    ky_src = ((1, 0), (0, 1), (1, 1), (0, 2))

    def patch(g, start, count):
        py, off = ky_src[g // 4]
        return ga_ref[g % 4, py, pl.ds(start + off * 128, count), :]

    def backward(it, carry):
        start = pl.multiple_of(it * step, step)
        total = None
        for pair in range(8):
            s = jnp.concatenate([patch(2 * pair, start, step), patch(2 * pair + 1, start, step)], axis=1)
            term = nt_dot(s, w4_ref[:, pair * 256 : (pair + 1) * 256])
            total = term if total is None else total + term
        total = total.astype(BF16)
        small_eye = eye[:c0, :c0]
        flipped = nt_dot(small_eye, total).astype(BF16)
        for k in range(step // 128):
            gin_ref[it * (step // 128) + k] = flipped[:, k * 128 : (k + 1) * 128]
        return carry

    xt = jnp.concatenate([x_ref[yc] for yc in range(yc_n)], axis=1)
    per, r = part.shape[2] // 2, part.shape[3]
    for pair in range(8):
        s = jnp.concatenate([patch(2 * pair, 0, pos), patch(2 * pair + 1, 0, pos)], axis=1)
        res = mm(xt, s)
        for h in range(2):
            part[pair // 4, pair % 4, h * per : (h + 1) * per] = (
                res[:, h * 128 : (h + 1) * 128].reshape(per, r, 128).astype(BF16)
            )

    pair_copies = [
        send(part.at[1 - core], r0, sems_c, 1, partner),
        send(sr0.at[core], sr0.at[core], sems_sc, 1, partner),
    ]
    half = pos // step // 4
    lax.fori_loop(0, half, backward, 0)
    for copy in pair_copies:
        copy.wait()
    m0[...] = (part[core].astype(F32) + r0[...].astype(F32)).astype(BF16)
    sm0[...] = sr0[0] + sr0[1]
    first = []
    for d in range(1, nb):
        to = lax.rem(mb + d, nb)
        first.append(send(m0.at[to], rb.at[mb], sems_b, d, (to, me)))
        first.append(send(sm0, srb.at[mb], sems_sb, d, (to, me)))
    rb[mb] = m0[mb]
    srb[mb] = sm0[...]
    lax.fori_loop(half, pos // step, backward, 0)
    for copy in first:
        copy.wait()
    acc = rb[0].astype(F32)
    sacc = srb[0]
    for b in range(1, nb):
        acc = acc + rb[b].astype(F32)
        sacc = sacc + srb[b]
    mid[...] = acc.astype(BF16)
    smid[...] = sacc
    second = []
    for d in range(1, nh):
        to = lax.rem(hs + d, nh)
        second.append(send(mid.at[to], rs.at[hs], sems_z, d, (mb, 2 * to + core)))
        second.append(send(smid, srs.at[hs], sems_sz, d, (mb, 2 * to + core)))
    rs[hs] = mid[hs]
    srs[hs] = sacc
    for copy in second:
        copy.wait()
    acc = rs[0].astype(F32)
    sacc = srs[0]
    for k in range(1, nh):
        acc = acc + rs[k].astype(F32)
        sacc = sacc + srs[k]
    osmall_ref[...] = sacc
    full[core, mb, hs] = acc.astype(BF16)
    third = []
    for d in range(1, nh):
        to = (mb, 2 * lax.rem(hs + d, nh) + core)
        third.append(send(full.at[core, mb, hs], full.at[core, mb, hs], sems_gz, d, to))
    for copy in third:
        copy.wait()
    fourth = []
    for d in range(1, nb):
        to = (lax.rem(mb + d, nb), me)
        fourth.append(send(full.at[core, mb], full.at[core, mb], sems_gb, d, to))
    for copy in fourth:
        copy.wait()
    send(full.at[core], full.at[core], sems_gc, 1, partner).wait()


def finish_kernel(scale, full_ref, osmall_ref, out_ref, ba_ref, wb_ref, bb_ref):
    c0 = out_ref.shape[0]
    per = full_ref.shape[2] // 2
    for ky in range(4):
        groups = [
            full_ref[ky // 2, 2 * (ky % 2) + kx // 2, (kx % 2) * per : (kx % 2 + 1) * per]
            .astype(F32)
            .reshape(c0, 128)
            * scale
            for kx in range(4)
        ]
        for kz in range(4):
            out_ref[:, kz * 512 + ky * 128 : kz * 512 + (ky + 1) * 128] = jnp.concatenate(
                [g[:, kz * 32 : (kz + 1) * 32] for g in groups], axis=1
            )
    tight = osmall_ref[...] * scale
    table = jnp.concatenate([tight[:, k * 32 : (k + 1) * 32] for k in range(4)], axis=0)
    eye = (
        lax.broadcasted_iota(jnp.int32, (32, 32), 0) == lax.broadcasted_iota(jnp.int32, (32, 32), 1)
    ).astype(F32)
    flipped = lax.dot_general(
        eye, table, (((1,), (1,)), ((), ())), precision=lax.Precision.HIGHEST,
        preferred_element_type=F32,
    )
    wb_ref[...] = flipped[:, 0:27]
    ba_ref[...] = table[27:28, :]
    bb_ref[...] = table[28:29, 0:1]


def body(nb, ns, activations, grad_image, pose_bin, shift, weight_a, bias_a, weight_b):
    vm = pl.BlockSpec(memory_space=pltpu.VMEM)
    _, c0, _, yc_n, xc_n = activations.shape
    c1 = bias_a.shape[0]
    pos = yc_n * xc_n
    x = activations[0, :, 0].transpose(1, 0, 2)
    img = grad_image[0]
    local_rows, width = img.shape
    angle = (pose_bin[0].astype(F32) + 0.5) * (math.pi / NBINS)
    trig = jnp.stack([jnp.cos(angle), jnp.sin(angle), shift[0].astype(F32)])
    nh = ns // 2
    r = 512 // (nb * nh)
    total_cells = nb * 2 * ns * 2 * yc_n * 2 * xc_n
    scale = 1.0 / math.sqrt(total_cells)
    gin, full, osmall = pl.pallas_call(
        functools.partial(local_kernel, nb, ns),
        out_shape=(
            jax.ShapeDtypeStruct((yc_n, c0, xc_n), BF16),
            jax.ShapeDtypeStruct((2, nb, nh, r, 128), BF16),
            jax.ShapeDtypeStruct((8, 128), F32),
        ),
        in_specs=[pl.BlockSpec(memory_space=pltpu.SMEM)] + [vm] * 5,
        out_specs=(vm, vm, vm),
        scratch_shapes=[
            pltpu.VMEM((3, pos + 256, 192), BF16),
            pltpu.VMEM((pos, 192), BF16),
            pltpu.VMEM((yc_n, 192, 128), BF16),
            pltpu.VMEM((4, 2, pos + 256, 128), BF16),
            pltpu.VMEM((2, 2, 3, 192, 256), BF16),
            pltpu.VMEM((c0, 2048), BF16),
            pltpu.VMEM((192, 512), BF16),
            pltpu.VMEM((pos, 512), BF16),
            pltpu.VMEM((2,) + x.shape, BF16),
            pltpu.VMEM((ns, local_rows, width), BF16),
            pltpu.SemaphoreType.DMA((2,)),
            pltpu.SemaphoreType.DMA((2,)),
            pltpu.SemaphoreType.DMA((ns - 1,)),
            pltpu.SemaphoreType.DMA((ns - 1,)),
            pltpu.VMEM((2, nb, nh, r, 128), BF16),
            pltpu.VMEM((nb, nh, r, 128), BF16),
            pltpu.VMEM((nb, nh, r, 128), BF16),
            pltpu.VMEM((nb, nh, r, 128), BF16),
            pltpu.VMEM((nh, r, 128), BF16),
            pltpu.VMEM((nh, r, 128), BF16),
            pltpu.VMEM((2, 8, 128), F32),
            pltpu.VMEM((8, 128), F32),
            pltpu.VMEM((nb, 8, 128), F32),
            pltpu.VMEM((8, 128), F32),
            pltpu.VMEM((nh, 8, 128), F32),
            pltpu.SemaphoreType.DMA((2, 1)),
            pltpu.SemaphoreType.DMA((2, nb - 1)),
            pltpu.SemaphoreType.DMA((2, nh - 1)),
            pltpu.SemaphoreType.DMA((2, nh - 1)),
            pltpu.SemaphoreType.DMA((2, nb - 1)),
            pltpu.SemaphoreType.DMA((2, 1)),
            pltpu.SemaphoreType.DMA((2, 1)),
            pltpu.SemaphoreType.DMA((2, nb - 1)),
            pltpu.SemaphoreType.DMA((2, nh - 1)),
        ],
        compiler_params=pltpu.CompilerParams(
            collective_id=0, has_side_effects=True, vmem_limit_bytes=VMEM_LIMIT
        ),
        name="local",
    )(
        trig, x, img, weight_a,
        bias_a.reshape(1, c1), weight_b,
    )
    grad_in = gin.transpose(1, 0, 2)[None, :, None]
    grad_wa, grad_ba, grad_wb, grad_bb = pl.pallas_call(
        functools.partial(finish_kernel, scale),
        out_shape=(
            jax.ShapeDtypeStruct(weight_a.shape, F32),
            jax.ShapeDtypeStruct((1, c1), F32),
            jax.ShapeDtypeStruct(weight_b.shape, F32),
            jax.ShapeDtypeStruct((1, 1), F32),
        ),
        in_specs=[vm, vm],
        out_specs=(vm, vm, vm, vm),
        compiler_params=pltpu.CompilerParams(vmem_limit_bytes=VMEM_LIMIT),
        name="finish",
    )(full, osmall)
    return (grad_in, grad_wa, grad_ba.reshape(c1), grad_wb, grad_bb.reshape(1))


def solution(mesh):
    return jax.shard_map(
        functools.partial(body, mesh.shape["batch"], mesh.shape["slab"]),
        mesh=mesh,
        in_specs=(
            P("batch", None, "slab", None, None),
            P("batch", "slab", None),
            P("batch"),
            P("batch"),
            P(),
            P(),
            P(),
        ),
        out_specs=(P("batch", None, "slab", None, None), P(), P(), P(), P()),
        check_vma=False,
    )
```

```python
import functools
import math

import jax
import jax.numpy as jnp
from jax import lax
from jax.experimental import pallas as pl
from jax.experimental.pallas import tpu as pltpu
from jax.sharding import PartitionSpec as P

NBINS = 32
MESH = pl.DeviceIdType.MESH
F32 = jnp.float32
BF16 = jnp.bfloat16
VMEM_LIMIT = 56 * 1024 * 1024


def nt_dot(a, b):
    return lax.dot_general(a, b, (((1,), (1,)), ((), ())), preferred_element_type=F32)


def mm(a, b):
    return jnp.dot(a, b, preferred_element_type=F32)


def local_kernel(
    nb,
    ns,
    trig_ref,
    x_ref,
    img_ref,
    wa_ref,
    bias_ref,
    taps_ref,
    gin_ref,
    full,
    osmall_ref,
    tt_ref,
    g_ref,
    gt_ref,
    ga_ref,
    wf_ref,
    w4_ref,
    wb_ref,
    act_ref,
    halo_ref,
    all_ref,
    h_send,
    h_recv,
    g_send,
    g_recv,
    part,
    r0,
    m0,
    rb,
    mid,
    rs,
    sr0,
    sm0,
    srb,
    smid,
    srs,
    sems_c,
    sems_b,
    sems_z,
    sems_gz,
    sems_gb,
    sems_gc,
    sems_sc,
    sems_sb,
    sems_sz,
):
    mb = lax.axis_index("batch")
    me = lax.axis_index("slab")
    nh = ns // 2
    core = lax.rem(me, 2)
    hs = me // 2
    partner = (mb, me + 1 - 2 * core)
    barrier = pltpu.get_barrier_semaphore()
    for d in range(1, nb):
        pl.semaphore_signal(barrier, inc=1, device_id=(lax.rem(mb + d, nb), me), device_id_type=MESH)
    for d in range(1, ns):
        peer = (mb, lax.rem(me + d, ns))
        pl.semaphore_signal(barrier, inc=1, device_id=peer, device_id_type=MESH)
    pl.semaphore_wait(barrier, nb + ns - 2)

    images = []
    for d in range(1, ns):
        copy = pltpu.make_async_remote_copy(
            src_ref=img_ref,
            dst_ref=all_ref.at[me],
            send_sem=g_send.at[d - 1],
            recv_sem=g_recv.at[d - 1],
            device_id=(mb, lax.rem(me + d, ns)),
            device_id_type=MESH,
        )
        copy.start()
        images.append(copy)

    def to_right():
        return pltpu.make_async_remote_copy(
            src_ref=x_ref,
            dst_ref=halo_ref.at[0],
            send_sem=h_send.at[0],
            recv_sem=h_recv.at[0],
            device_id=(mb, lax.rem(me + 1, ns)),
            device_id_type=MESH,
        )

    def to_left():
        return pltpu.make_async_remote_copy(
            src_ref=x_ref,
            dst_ref=halo_ref.at[1],
            send_sem=h_send.at[1],
            recv_sem=h_recv.at[1],
            device_id=(mb, lax.rem(me + ns - 1, ns)),
            device_id_type=MESH,
        )

    @pl.when(me < ns - 1)
    def _():
        to_right().start()

    @pl.when(me > 0)
    def _():
        to_left().start()

    all_ref[me] = img_ref[...]

    @pl.when(me == 0)
    def _():
        halo_ref[0] = jnp.zeros(halo_ref.shape[1:], halo_ref.dtype)

    @pl.when(me == ns - 1)
    def _():
        halo_ref[1] = jnp.zeros(halo_ref.shape[1:], halo_ref.dtype)

    def send(src, dst, sems, d, device):
        copy = pltpu.make_async_remote_copy(
            src_ref=src,
            dst_ref=dst,
            send_sem=sems.at[0, d - 1],
            recv_sem=sems.at[1, d - 1],
            device_id=device,
            device_id_type=MESH,
        )
        copy.start()
        return copy

    yc_n, c0, xc_n = x_ref.shape
    c1 = 32
    rows = ns * img_ref.shape[0]
    depth = 2 * ns
    height = 2 * yc_n
    pos = yc_n * xc_n

    def iota(shape, dim):
        return lax.broadcasted_iota(jnp.int32, shape, dim)

    w = wa_ref[...]
    lane = iota((c0, 128), 1)
    for g in range(16):
        block = jnp.concatenate(
            [w[:, kz * 512 + g * 32 : kz * 512 + g * 32 + 32] for kz in range(4)], axis=1
        )
        w4_ref[:, g * 128 : (g + 1) * 128] = block
    zero_block = jnp.zeros((c0, 128), BF16)
    for py in range(2):
        for dyi in range(2):
            dy = py - 1 + dyi
            ky = py - 2 * dy + 1
            for dxi in range(3):
                dx = dxi - 1
                for px in range(2):
                    kx = px - 2 * dx + 1
                    for plane in range(3):
                        if 0 <= kx <= 3:
                            g = ky * 4 + kx
                            base = w4_ref[:, g * 128 : (g + 1) * 128]
                            half = jnp.zeros((c0, 64), BF16)
                            if plane == 0:
                                base = jnp.concatenate([base[:, 64:], half], axis=1)
                            elif plane == 2:
                                base = jnp.concatenate([half, base[:, :64]], axis=1)
                        else:
                            base = zero_block
                        wf_ref[
                            py, dyi, dxi, plane * c0 : (plane + 1) * c0, px * 128 : (px + 1) * 128
                        ] = base

    row = iota((96, 512), 0)
    col = iota((96, 512), 1)
    q = col >> 5
    tz, px_c, py_c = (q & 3, (q >> 2) & 1, (q >> 3) & 1)
    tx_r = (
        (row >= 24).astype(jnp.int32)
        + (row >= 48).astype(jnp.int32)
        + (row >= 72).astype(jnp.int32)
    )
    rem = row - 24 * tx_r
    az = (rem >> 2) - tz
    by = (rem & 3) - py_c
    cx = tx_r - px_c
    ok = (az >= 0) & (az < 3) & (by >= 0) & (by < 3) & (cx >= 0) & (cx < 3)
    index = jnp.where(ok, 9 * az + 3 * by + cx, -1)
    inside = ((tz > 0) | (me > 0)) & ((tz < 3) | (me < ns - 1))
    masked_index = jnp.where(inside, index, -1)
    spread = (iota((c1, 512), 0) == (iota((c1, 512), 1) & 31)).astype(F32).astype(BF16)
    eye_t = (iota((27, 27), 0) == iota((27, 27), 1)).astype(F32).astype(BF16)
    wbt = mm(nt_dot(eye_t, taps_ref[...]).astype(BF16), spread)
    wb_mat = jnp.zeros((96, 512), F32)
    for t in range(27):
        wb_mat = jnp.where(masked_index == t, wbt[t : t + 1, :], wb_mat)
    wb_mat = wb_mat.astype(BF16)
    wb_ref[0:96, :] = wb_mat
    wb_ref[96:192, :] = wb_mat

    width = img_ref.shape[1]
    col_x = iota((width, 512), 1)
    fine = 2 * (col_x & 127) + (col_x >> 7) - 1
    sel = (iota((width, 512), 0) == fine).astype(F32).astype(BF16)
    for copy in images:
        copy.wait()
    whole_image = all_ref[...].astype(F32).reshape(rows, width).astype(BF16)
    ims = mm(whole_image, sel).astype(BF16)
    shape3 = (yc_n, 24, rows)
    j = iota(shape3, 1)
    y = 2 * iota(shape3, 0) + (j & 3) - 1
    z = 2 * me - 2 + (j >> 2)
    center = (
        (y.astype(F32) - 0.5 * (height - 1)) * trig_ref[0]
        + (z.astype(F32) - 0.5 * (depth - 1)) * trig_ref[1]
        + (0.5 * (rows - 1) + trig_ref[2])
    )
    interp = jnp.maximum(1.0 - jnp.abs(iota(shape3, 2).astype(F32) - center), 0.0)
    interp = jnp.where((y >= 0) & (y < height) & (z >= 0) & (z < depth), interp, 0.0)
    interp = interp.reshape(yc_n * 24, rows)
    hi = interp.astype(BF16)
    lo = (interp - hi.astype(F32)).astype(BF16)
    gtf = mm(hi, ims) + mm(lo, ims)
    eye = (iota((128, 128), 0) == iota((128, 128), 1)).astype(F32).astype(BF16)
    own_rows = iota((24, 256), 0)
    own = ((own_rows >> 2) >= 2) & ((own_rows >> 2) < 4) & ((own_rows & 3) > 0) & ((own_rows & 3) < 3)
    gb_total = jnp.zeros((24, 256), F32)
    sh_row = iota((384, 128), 0)
    shift_mat = (
        iota((384, 128), 1) == (sh_row & 127) + (sh_row >> 7) - 1
    ).astype(F32).astype(BF16)
    pad = jnp.zeros((128, 192), BF16)
    for dxi in range(3):
        tt_ref[dxi, 0:128, :] = pad
        tt_ref[dxi, pos + 128 : pos + 256, :] = pad
    for yc in range(yc_n):
        f = gtf[yc * 24 : (yc + 1) * 24]
        gb_total = gb_total + jnp.where(own, f[:, 128:384], 0.0)
        blk = jnp.concatenate([f[:, tx * 128 : (tx + 1) * 128] for tx in range(4)], axis=0)
        bhi = blk.astype(BF16)
        blo = (blk - bhi.astype(F32)).astype(BF16)
        gt = jnp.concatenate([bhi, blo], axis=0)
        gt_ref[yc] = gt
        g_ref[yc * 128 : (yc + 1) * 128, :] = nt_dot(eye, gt).astype(BF16)

    @pl.when(me < ns - 1)
    def _():
        to_right().wait_send()
        to_left().wait_recv()

    @pl.when(me > 0)
    def _():
        to_left().wait_send()
        to_right().wait_recv()

    for yc in range(yc_n):
        planes = jnp.concatenate([halo_ref[0, yc], x_ref[yc], halo_ref[1, yc]], axis=0)
        r = nt_dot(shift_mat, planes).astype(BF16)
        for dxi in range(3):
            tt_ref[dxi, (yc + 1) * 128 : (yc + 2) * 128, :] = r[dxi * 128 : (dxi + 1) * 128]

    zpad = jnp.zeros((128, 128), BF16)
    for kx in range(4):
        for py in range(2):
            ga_ref[kx, py, 0:128, :] = zpad
            ga_ref[kx, py, pos + 128 : pos + 256, :] = zpad
    step = 512
    xc_id = iota((step, 128), 0) & 127
    bias = jnp.concatenate([bias_ref[...]] * 8, axis=1)

    def forward(it, sums):
        start = pl.multiple_of(it * step, step)
        new = []
        for py in range(2):
            pre = None
            for dyi in range(2):
                for dxi in range(3):
                    base = pl.multiple_of(start + (py + dyi) * 128, 128)
                    term = mm(tt_ref[dxi, pl.ds(base, step), :], wf_ref[py, dyi, dxi])
                    pre = term if pre is None else pre + term
            pre = pre + bias
            raw = mm(g_ref[pl.ds(start, step), :], wb_ref[:, py * 256 : (py + 1) * 256])
            gate = 0.5 * jnp.tanh(0.5 * pre) + 0.5
            act = pre * gate
            ga = (gate + act * (1.0 - gate)) * raw
            act_ref[pl.ds(start, step), py * 256 : (py + 1) * 256] = act.astype(BF16)
            new.append(sums[py] + jnp.sum(ga.reshape(step // 8, 8, 256), axis=0))
            dst = pl.ds(pl.multiple_of(start + 128, 128), step)
            g0, g1 = ga[:, :128], ga[:, 128:]
            ga_ref[1, py, dst, :] = g0.astype(BF16)
            ga_ref[2, py, dst, :] = g1.astype(BF16)
            ga_ref[0, py, dst, :] = jnp.where(xc_id == 0, 0.0, pltpu.roll(g1, 1, 0)).astype(BF16)
            ga_ref[3, py, dst, :] = jnp.where(
                xc_id == 127, 0.0, pltpu.roll(g0, step - 1, 0)
            ).astype(BF16)
        return tuple(new)

    zero_sum = jnp.zeros((8, 256), F32)
    sums = lax.fori_loop(0, pos // step, forward, (zero_sum, zero_sum))

    r_mat = jnp.zeros((192, 512), F32)
    for yc in range(yc_n):
        r_mat = r_mat + mm(gt_ref[yc], act_ref[yc * 128 : (yc + 1) * 128, :])
    r_sum = r_mat[0:96] + r_mat[96:192]
    mine = (tz > 0) & (tz < 3)
    own_index = jnp.where(mine, index, -1)
    lines = []
    for t in range(27):
        lines.append(jnp.sum(jnp.where(own_index == t, r_sum, 0.0), axis=0, keepdims=True))
    ba_row = jnp.sum(jnp.concatenate([sums[0], sums[1]], axis=1), axis=0, keepdims=True)
    lane5 = iota((1, 512), 1)
    tz5 = (lane5 >> 5) & 3
    lines.append(jnp.where((tz5 > 0) & (tz5 < 3), ba_row, 0.0))
    bb_total = jnp.sum(jnp.sum(gb_total, axis=0, keepdims=True), axis=1, keepdims=True)
    lines.append(jnp.where(lane5 == 0, bb_total, 0.0))
    lines.append(jnp.zeros((3, 512), F32))
    packed = jnp.concatenate(lines, axis=0)
    fold = packed[:, 0:128] + packed[:, 128:256] + packed[:, 256:384] + packed[:, 384:512]
    fold = fold + pltpu.roll(fold, 64, 1)
    fold = fold + pltpu.roll(fold, 32, 1)
    group = iota((8, 128), 1) >> 5
    tight = fold[0:8]
    for k in range(1, 4):
        tight = jnp.where(group == k, fold[8 * k : 8 * k + 8], tight)
    sr0[core] = tight

    ky_src = ((1, 0), (0, 1), (1, 1), (0, 2))

    def patch(g, start, count):
        py, off = ky_src[g // 4]
        return ga_ref[g % 4, py, pl.ds(start + off * 128, count), :]

    def backward(it, carry):
        start = pl.multiple_of(it * step, step)
        total = None
        for pair in range(8):
            s = jnp.concatenate([patch(2 * pair, start, step), patch(2 * pair + 1, start, step)], axis=1)
            term = nt_dot(s, w4_ref[:, pair * 256 : (pair + 1) * 256])
            total = term if total is None else total + term
        total = total.astype(BF16)
        small_eye = eye[:c0, :c0]
        flipped = nt_dot(small_eye, total).astype(BF16)
        for k in range(step // 128):
            gin_ref[it * (step // 128) + k] = flipped[:, k * 128 : (k + 1) * 128]
        return carry

    xt = jnp.concatenate([x_ref[yc] for yc in range(yc_n)], axis=1)
    per, r = part.shape[2] // 2, part.shape[3]
    for pair in range(8):
        s = jnp.concatenate([patch(2 * pair, 0, pos), patch(2 * pair + 1, 0, pos)], axis=1)
        res = mm(xt, s)
        for h in range(2):
            part[pair // 4, pair % 4, h * per : (h + 1) * per] = (
                res[:, h * 128 : (h + 1) * 128].reshape(per, r, 128).astype(BF16)
            )

    pair_copies = [
        send(part.at[1 - core], r0, sems_c, 1, partner),
        send(sr0.at[core], sr0.at[core], sems_sc, 1, partner),
    ]
    half = pos // step // 4
    lax.fori_loop(0, half, backward, 0)
    for copy in pair_copies:
        copy.wait()
    m0[...] = (part[core].astype(F32) + r0[...].astype(F32)).astype(BF16)
    sm0[...] = sr0[0] + sr0[1]
    first = []
    for d in range(1, nb):
        to = lax.rem(mb + d, nb)
        first.append(send(m0.at[to], rb.at[mb], sems_b, d, (to, me)))
        first.append(send(sm0, srb.at[mb], sems_sb, d, (to, me)))
    rb[mb] = m0[mb]
    srb[mb] = sm0[...]
    lax.fori_loop(half, pos // step, backward, 0)
    for copy in first:
        copy.wait()
    acc = rb[0].astype(F32)
    sacc = srb[0]
    for b in range(1, nb):
        acc = acc + rb[b].astype(F32)
        sacc = sacc + srb[b]
    mid[...] = acc.astype(BF16)
    smid[...] = sacc
    second = []
    for d in range(1, nh):
        to = lax.rem(hs + d, nh)
        second.append(send(mid.at[to], rs.at[hs], sems_z, d, (mb, 2 * to + core)))
        second.append(send(smid, srs.at[hs], sems_sz, d, (mb, 2 * to + core)))
    rs[hs] = mid[hs]
    srs[hs] = sacc
    for copy in second:
        copy.wait()
    acc = rs[0].astype(F32)
    sacc = srs[0]
    for k in range(1, nh):
        acc = acc + rs[k].astype(F32)
        sacc = sacc + srs[k]
    osmall_ref[...] = sacc
    full[core, mb, hs] = acc.astype(BF16)
    third = []
    for d in range(1, nh):
        to = (mb, 2 * lax.rem(hs + d, nh) + core)
        third.append(send(full.at[core, mb, hs], full.at[core, mb, hs], sems_gz, d, to))
    for copy in third:
        copy.wait()
    fourth = []
    for d in range(1, nb):
        to = (lax.rem(mb + d, nb), me)
        fourth.append(send(full.at[core, mb], full.at[core, mb], sems_gb, d, to))
    fifth = [send(full.at[core, mb], full.at[core, mb], sems_gc, 1, partner)]
    for d in range(1, nb):
        fourth[d - 1].wait()
        came = full.at[core, lax.rem(mb + nb - d, nb)]
        fifth.append(send(came, came, sems_gc, d + 1, partner))
    for copy in fifth:
        copy.wait()


def finish_kernel(scale, full_ref, osmall_ref, out_ref, ba_ref, wb_ref, bb_ref):
    c0 = out_ref.shape[0]
    per = full_ref.shape[2] // 2
    for ky in range(4):
        groups = [
            full_ref[ky // 2, 2 * (ky % 2) + kx // 2, (kx % 2) * per : (kx % 2 + 1) * per]
            .astype(F32)
            .reshape(c0, 128)
            * scale
            for kx in range(4)
        ]
        for kz in range(4):
            out_ref[:, kz * 512 + ky * 128 : kz * 512 + (ky + 1) * 128] = jnp.concatenate(
                [g[:, kz * 32 : (kz + 1) * 32] for g in groups], axis=1
            )
    tight = osmall_ref[...] * scale
    table = jnp.concatenate([tight[:, k * 32 : (k + 1) * 32] for k in range(4)], axis=0)
    eye = (
        lax.broadcasted_iota(jnp.int32, (32, 32), 0) == lax.broadcasted_iota(jnp.int32, (32, 32), 1)
    ).astype(F32)
    flipped = lax.dot_general(
        eye, table, (((1,), (1,)), ((), ())), precision=lax.Precision.HIGHEST,
        preferred_element_type=F32,
    )
    wb_ref[...] = flipped[:, 0:27]
    ba_ref[...] = table[27:28, :]
    bb_ref[...] = table[28:29, 0:1]


def body(nb, ns, activations, grad_image, pose_bin, shift, weight_a, bias_a, weight_b):
    vm = pl.BlockSpec(memory_space=pltpu.VMEM)
    _, c0, _, yc_n, xc_n = activations.shape
    c1 = bias_a.shape[0]
    pos = yc_n * xc_n
    x = activations[0, :, 0].transpose(1, 0, 2)
    img = grad_image[0]
    local_rows, width = img.shape
    angle = (pose_bin[0].astype(F32) + 0.5) * (math.pi / NBINS)
    trig = jnp.stack([jnp.cos(angle), jnp.sin(angle), shift[0].astype(F32)])
    nh = ns // 2
    r = 512 // (nb * nh)
    total_cells = nb * 2 * ns * 2 * yc_n * 2 * xc_n
    scale = 1.0 / math.sqrt(total_cells)
    gin, full, osmall = pl.pallas_call(
        functools.partial(local_kernel, nb, ns),
        out_shape=(
            jax.ShapeDtypeStruct((yc_n, c0, xc_n), BF16),
            jax.ShapeDtypeStruct((2, nb, nh, r, 128), BF16),
            jax.ShapeDtypeStruct((8, 128), F32),
        ),
        in_specs=[pl.BlockSpec(memory_space=pltpu.SMEM)] + [vm] * 5,
        out_specs=(vm, vm, vm),
        scratch_shapes=[
            pltpu.VMEM((3, pos + 256, 192), BF16),
            pltpu.VMEM((pos, 192), BF16),
            pltpu.VMEM((yc_n, 192, 128), BF16),
            pltpu.VMEM((4, 2, pos + 256, 128), BF16),
            pltpu.VMEM((2, 2, 3, 192, 256), BF16),
            pltpu.VMEM((c0, 2048), BF16),
            pltpu.VMEM((192, 512), BF16),
            pltpu.VMEM((pos, 512), BF16),
            pltpu.VMEM((2,) + x.shape, BF16),
            pltpu.VMEM((ns, local_rows, width), BF16),
            pltpu.SemaphoreType.DMA((2,)),
            pltpu.SemaphoreType.DMA((2,)),
            pltpu.SemaphoreType.DMA((ns - 1,)),
            pltpu.SemaphoreType.DMA((ns - 1,)),
            pltpu.VMEM((2, nb, nh, r, 128), BF16),
            pltpu.VMEM((nb, nh, r, 128), BF16),
            pltpu.VMEM((nb, nh, r, 128), BF16),
            pltpu.VMEM((nb, nh, r, 128), BF16),
            pltpu.VMEM((nh, r, 128), BF16),
            pltpu.VMEM((nh, r, 128), BF16),
            pltpu.VMEM((2, 8, 128), F32),
            pltpu.VMEM((8, 128), F32),
            pltpu.VMEM((nb, 8, 128), F32),
            pltpu.VMEM((8, 128), F32),
            pltpu.VMEM((nh, 8, 128), F32),
            pltpu.SemaphoreType.DMA((2, 1)),
            pltpu.SemaphoreType.DMA((2, nb - 1)),
            pltpu.SemaphoreType.DMA((2, nh - 1)),
            pltpu.SemaphoreType.DMA((2, nh - 1)),
            pltpu.SemaphoreType.DMA((2, nb - 1)),
            pltpu.SemaphoreType.DMA((2, nb)),
            pltpu.SemaphoreType.DMA((2, 1)),
            pltpu.SemaphoreType.DMA((2, nb - 1)),
            pltpu.SemaphoreType.DMA((2, nh - 1)),
        ],
        compiler_params=pltpu.CompilerParams(
            collective_id=0, has_side_effects=True, vmem_limit_bytes=VMEM_LIMIT
        ),
        name="local",
    )(
        trig, x, img, weight_a,
        bias_a.reshape(1, c1), weight_b,
    )
    grad_in = gin.transpose(1, 0, 2)[None, :, None]
    grad_wa, grad_ba, grad_wb, grad_bb = pl.pallas_call(
        functools.partial(finish_kernel, scale),
        out_shape=(
            jax.ShapeDtypeStruct(weight_a.shape, F32),
            jax.ShapeDtypeStruct((1, c1), F32),
            jax.ShapeDtypeStruct(weight_b.shape, F32),
            jax.ShapeDtypeStruct((1, 1), F32),
        ),
        in_specs=[vm, vm],
        out_specs=(vm, vm, vm, vm),
        compiler_params=pltpu.CompilerParams(vmem_limit_bytes=VMEM_LIMIT),
        name="finish",
    )(full, osmall)
    return (grad_in, grad_wa, grad_ba.reshape(c1), grad_wb, grad_bb.reshape(1))


def solution(mesh):
    return jax.shard_map(
        functools.partial(body, mesh.shape["batch"], mesh.shape["slab"]),
        mesh=mesh,
        in_specs=(
            P("batch", None, "slab", None, None),
            P("batch", "slab", None),
            P("batch"),
            P("batch"),
            P(),
            P(),
            P(),
        ),
        out_specs=(P("batch", None, "slab", None, None), P(), P(), P(), P()),
        check_vma=False,
    )
```
